32 devices in a mesh: seq: 8 (over y, x, core), chan: 4 (over z).
Axes of the slice: x: 2, y: 2, z: 4, core: 2. Of those that a mesh axis runs over, the one named last changes fastest.
Arguments:
- queries: bfloat16 [64, 32768], P('chan', 'seq'), may hold values from -6 to 6
- key_proj: bfloat16 [64, 32768], P('chan', 'seq'), may hold values from -6 to 6
- value_proj: bfloat16 [64, 32768], P('chan', 'seq'), may hold values from -6 to 6
- cotangent: bfloat16 [64, 32768], P('chan', 'seq'), may hold values from -6 to 6
- filter_taps: bfloat16 [64, 32768], P('chan', 'seq'), may hold values from -0.032958984 to 0.032958984
- skip_gain: float32 [64], P('chan'), may hold values from -6 to 6
Outputs:
- grad_query: bfloat16 [64, 32768], P('chan', 'seq')
- grad_key: bfloat16 [64, 32768], P('chan', 'seq')
- grad_value: bfloat16 [64, 32768], P('chan', 'seq')
- grad_filter: bfloat16 [64, 32768], P('chan', 'seq')
- grad_skip: float32 [64], P('chan')
The draws below stay inside these ranges and needn't reach their ends.
All inputs are finite; a program needn't handle non-finite values.
Results may differ from the reference program's by a relative error of at most 0.001.
Values may be sent and summed in bfloat16 or wider, within the bound.
A program may use at most 64 MiB of HBM per device.

```python
import math
import jax
import jax.numpy as jnp
from jax import lax

SLAB = 64
TOKENS = 32768


def block_levels(own_key, dims, pieces, least, high):
    def one(position, parts):
        heights = jax.random.uniform(jax.random.fold_in(jax.random.fold_in(own_key, 6), position), (parts,), jnp.float32, least / len(pieces), high / len(pieces))
        return jnp.repeat(jnp.exp(heights), dims[position] // parts).reshape((-1,) + (1,) * (len(dims) - position - 1))

    loudness = one(*pieces[0])
    for cut in pieces[1:]:
        loudness = loudness * one(*cut)
    return loudness


def scatter_about(own_key, dims, spread, most, pieces=(), kind=jnp.bfloat16):
    array = jax.random.normal(own_key, dims, jnp.float32) * spread
    if len(pieces) > 0:
        array = block_levels(own_key, dims, pieces, -0.22, 0.18) * array
    return jnp.clip(array, min=-most, max=most).astype(kind)


def setup_inputs(seed: int = 0) -> dict:
    key_of = jax.random.split(jax.random.key(seed), 7)
    queries = scatter_about(key_of[0], (SLAB, TOKENS), 1.0, 6.0, ((0, 4), (1, 8)))
    key_proj = scatter_about(key_of[1], (SLAB, TOKENS), 1.0, 6.0, ((0, 4), (1, 8)))
    value_proj = scatter_about(key_of[2], (SLAB, TOKENS), 1.0, 6.0, ((0, 4), (1, 8)))
    cotangent = scatter_about(key_of[3], (SLAB, TOKENS), 1.0, 6.0, ((0, 4), (1, 8)))
    filter_taps = scatter_about(key_of[4], (SLAB, TOKENS), (1.0 / TOKENS ** 0.5), 0.032958984, ((0, 4), (1, 8)))
    skip_gain = scatter_about(key_of[5], (SLAB,), 1.0, 6.0, ((0, 4),), jnp.float32)
    return dict(queries=queries, key_proj=key_proj, value_proj=value_proj, cotangent=cotangent, filter_taps=filter_taps, skip_gain=skip_gain)


def channel_group(packed):
    queries, key_proj, value_proj, cotangent, filter_taps, skip_gain = packed
    tokens_all = queries.shape[-1]
    padded_len = 2 * tokens_all
    norm_scale = 1.0 / math.sqrt(tokens_all)
    query_f = queries.astype(jnp.float32)
    key_f = key_proj.astype(jnp.float32)
    value_f = value_proj.astype(jnp.float32)
    cot_f = cotangent.astype(jnp.float32)
    kernel = filter_taps.astype(jnp.float32)
    mixed = key_f * value_f
    gated = cot_f * query_f
    mix_spec = jnp.fft.rfft(mixed, n=padded_len, axis=-1)
    grad_spec = jnp.fft.rfft(gated, n=padded_len, axis=-1)
    ker_spec = jnp.fft.rfft(kernel, n=padded_len, axis=-1)
    convolved = jnp.fft.irfft(ker_spec * mix_spec, n=padded_len, axis=-1)[:, :tokens_all]
    carried = jnp.fft.irfft(jnp.conj(ker_spec) * grad_spec, n=padded_len, axis=-1)[:, :tokens_all]
    lag_grad = jnp.fft.irfft(grad_spec * jnp.conj(mix_spec), n=padded_len, axis=-1)[:, :tokens_all]
    skip_col = skip_gain[:, None]
    grad_query = (cot_f * (convolved + skip_col * mixed)).astype(jnp.bfloat16)
    grad_mixed = carried + skip_col * gated
    grad_key = (grad_mixed * value_f).astype(jnp.bfloat16)
    grad_value = (grad_mixed * key_f).astype(jnp.bfloat16)
    grad_filter = (lag_grad * norm_scale).astype(jnp.bfloat16)
    skip_part = lax.optimization_barrier(jnp.sum(gated * mixed, axis=1))
    return (grad_query, grad_key, grad_value, grad_filter, skip_part)

def reference(queries, key_proj, value_proj, cotangent, filter_taps, skip_gain):
    groups = SLAB // 8
    packed = (queries.reshape(groups, 8, TOKENS), key_proj.reshape(groups, 8, TOKENS), value_proj.reshape(groups, 8, TOKENS), cotangent.reshape(groups, 8, TOKENS), filter_taps.reshape(groups, 8, TOKENS), skip_gain.reshape(groups, 8))
    grad_query, grad_key, grad_value, grad_filter, skip_part = lax.map(channel_group, packed)
    norm_scale = 1.0 / math.sqrt(TOKENS)
    return (grad_query.reshape(SLAB, TOKENS), grad_key.reshape(SLAB, TOKENS), grad_value.reshape(SLAB, TOKENS), grad_filter.reshape(SLAB, TOKENS), skip_part.reshape(SLAB) * norm_scale)
```

```python
import functools
import math

import jax
import jax.numpy as jnp
import ml_dtypes
import numpy as np
from jax import lax
from jax.experimental import pallas as pl
from jax.experimental.pallas import tpu as pltpu
from jax.sharding import PartitionSpec as P

highest = lax.Precision.HIGHEST


def from_partner(block, axis, stride):
    count = lax.axis_size(axis)
    route = []
    for low in range(count):
        high = low | 1 << stride
        if high != low and high < count:
            route += [(low, high), (high, low)]
    return lax.ppermute(block, axis, route)


def complex_product(pattern, left_re, left_im, right_re, right_im):
    real_real = jnp.einsum(pattern, left_re, right_re, precision=highest)
    imag_imag = jnp.einsum(pattern, left_im, right_im, precision=highest)
    real_imag = jnp.einsum(pattern, left_re, right_im, precision=highest)
    imag_real = jnp.einsum(pattern, left_im, right_re, precision=highest)
    return (real_real - imag_imag, real_imag + imag_real)


def rotate(real_in, imag_in, angle_val):
    cosine = jnp.cos(angle_val)
    sine_val = jnp.sin(angle_val)
    return (real_in * cosine - imag_in * sine_val, real_in * sine_val + imag_in * cosine)


def dft_table(length, direction):
    counter = jnp.arange(length, dtype=jnp.int32)
    phase_idx = counter[:, None] * counter[None, :] % length
    angle_val = direction * 2.0 * math.pi / length * phase_idx.astype(jnp.float32)
    return (jnp.cos(angle_val), jnp.sin(angle_val))


def twiddle_angle(row_count, radix_len, length, direction):
    phase_idx = (
        jnp.arange(row_count, dtype=jnp.int32)[:, None]
        * jnp.arange(radix_len, dtype=jnp.int32)[None, :]
        % length
    )
    return direction * 2.0 * math.pi / length * phase_idx.astype(jnp.float32)


def local_forward(real_in, imag_in):
    length = real_in.shape[-1]
    radix_len = math.gcd(length, 512)
    row_count = length // radix_len
    new_shape = real_in.shape[:-1] + (row_count, radix_len)
    first_re, first_im = dft_table(row_count, -1.0)
    work_re, work_im = complex_product(
        "ab,...bj->...aj",
        first_re,
        first_im,
        real_in.reshape(new_shape),
        imag_in.reshape(new_shape),
    )
    work_re, work_im = rotate(work_re, work_im, twiddle_angle(row_count, radix_len, length, -1.0))
    second_re, second_im = dft_table(radix_len, -1.0)
    work_re, work_im = complex_product("...aj,jk->...ak", work_re, work_im, second_re, second_im)
    return (work_re.reshape(real_in.shape), work_im.reshape(real_in.shape))


def local_inverse(real_in, imag_in):
    length = real_in.shape[-1]
    radix_len = math.gcd(length, 512)
    row_count = length // radix_len
    new_shape = real_in.shape[:-1] + (row_count, radix_len)
    second_re, second_im = dft_table(radix_len, 1.0)
    work_re, work_im = complex_product(
        "...ak,kj->...aj",
        real_in.reshape(new_shape),
        imag_in.reshape(new_shape),
        second_re,
        second_im,
    )
    work_re, work_im = rotate(work_re, work_im, twiddle_angle(row_count, radix_len, length, 1.0))
    first_re, first_im = dft_table(row_count, 1.0)
    work_re, work_im = complex_product("ab,...aj->...bj", first_re, first_im, work_re, work_im)
    return (work_re.reshape(real_in.shape), work_im.reshape(real_in.shape))


def bit_reverse(seq_index, bit_total):
    reversed_idx = jnp.zeros_like(seq_index)
    for bit_level in range(bit_total):
        reversed_idx = reversed_idx | (seq_index >> bit_level & 1) << bit_total - 1 - bit_level
    return reversed_idx


def frequency_angle(frequencies, lane_count, padded_len, direction):
    lanes = jnp.arange(lane_count, dtype=jnp.int32)
    parity = jnp.arange(2, dtype=jnp.int32)
    spectral = 2 * frequencies[None, :] + parity[:, None]
    phase_idx = spectral[:, :, None] * lanes[None, None, :] % padded_len
    angle_val = direction * 2.0 * math.pi / padded_len * phase_idx.astype(jnp.float32)
    return angle_val[:, None, None]


def to_spectrum(signals, blocks, seq_index, seq_count, block_total):
    lane_count = signals.shape[-1]
    padded_len = 2 * block_total * lane_count
    half_turn = (math.pi / block_total * blocks.astype(jnp.float32))[:, None]
    real_part = jnp.stack([signals, signals * jnp.cos(half_turn)])
    imag_part = jnp.stack([jnp.zeros_like(signals), -signals * jnp.sin(half_turn)])
    bit_total = seq_count.bit_length() - 1
    for bit_level in reversed(range(bit_total)):
        half_span = 1 << bit_level
        other_re, other_im = from_partner((real_part, imag_part), "seq", bit_level)
        position = seq_index % (2 * half_span)
        is_upper = position < half_span
        sum_re = jnp.where(is_upper, real_part + other_re, other_re - real_part)
        sum_im = jnp.where(is_upper, imag_part + other_im, other_im - imag_part)
        angle_val = jnp.where(
            is_upper, 0.0, -math.pi * (position % half_span).astype(jnp.float32) / half_span
        )
        real_part, imag_part = rotate(sum_re, sum_im, angle_val)
    frequencies = bit_reverse(seq_index, bit_total)[None]
    real_part, imag_part = rotate(
        real_part, imag_part, frequency_angle(frequencies, lane_count, padded_len, -1.0)
    )
    return (local_forward(real_part, imag_part), frequencies)


def to_signal(real_part, imag_part, frequencies, blocks, seq_index, seq_count, block_total):
    lane_count = real_part.shape[-1]
    padded_len = 2 * block_total * lane_count
    real_part, imag_part = local_inverse(real_part, imag_part)
    real_part, imag_part = rotate(
        real_part, imag_part, frequency_angle(frequencies, lane_count, padded_len, 1.0)
    )
    bit_total = seq_count.bit_length() - 1
    for bit_level in range(bit_total):
        half_span = 1 << bit_level
        other_re, other_im = from_partner((real_part, imag_part), "seq", bit_level)
        position = seq_index % (2 * half_span)
        is_upper = position < half_span
        taken_re = jnp.where(is_upper, other_re, real_part)
        taken_im = jnp.where(is_upper, other_im, imag_part)
        base_re = jnp.where(is_upper, real_part, other_re)
        base_im = jnp.where(is_upper, imag_part, other_im)
        angle_val = math.pi * (position % half_span).astype(jnp.float32) / half_span
        turned_re, turned_im = rotate(taken_re, taken_im, angle_val)
        flip_sign = jnp.where(is_upper, 1.0, -1.0)
        real_part = base_re + flip_sign * turned_re
        imag_part = base_im + flip_sign * turned_im
    half_turn = (math.pi / block_total * blocks.astype(jnp.float32))[:, None]
    combined = real_part[0] + real_part[1] * jnp.cos(half_turn) - imag_part[1] * jnp.sin(half_turn)
    return combined / padded_len


def local_butterfly(queries, key_proj, value_proj, cotangent, filter_taps, skip_gain):
    seq_count = lax.axis_size("seq")
    seq_index = lax.axis_index("seq")
    tok_local = queries.shape[1]
    tokens_all = seq_count * tok_local
    norm_scale = 1.0 / math.sqrt(tokens_all)
    chan_input = queries.shape[0]
    query_in, key_in, value_in, cot_in, taps_in = (
        queries,
        key_proj,
        value_proj,
        cotangent,
        filter_taps,
    )
    blocks = seq_index[None]
    block_shape = (chan_input, blocks.shape[0], tok_local)
    query_f = query_in.reshape(block_shape).astype(jnp.float32)
    key_f = key_in.reshape(block_shape).astype(jnp.float32)
    value_f = value_in.reshape(block_shape).astype(jnp.float32)
    cot_f = cot_in.reshape(block_shape).astype(jnp.float32)
    kernel = taps_in.reshape(block_shape).astype(jnp.float32)
    mixed = key_f * value_f
    gated = cot_f * query_f
    signals = jnp.stack([mixed, gated, kernel])
    (spec_re, spec_im), frequencies = to_spectrum(signals, blocks, seq_index, seq_count, seq_count)
    mix_re, mix_im = (spec_re[:, 0], spec_im[:, 0])
    grad_re, grad_im = (spec_re[:, 1], spec_im[:, 1])
    ker_re, ker_im = (spec_re[:, 2], spec_im[:, 2])
    prod_re = jnp.stack(
        [
            ker_re * mix_re - ker_im * mix_im,
            ker_re * grad_re + ker_im * grad_im,
            grad_re * mix_re + grad_im * mix_im,
        ],
        1,
    )
    prod_im = jnp.stack(
        [
            ker_re * mix_im + ker_im * mix_re,
            ker_re * grad_im - ker_im * grad_re,
            grad_im * mix_re - grad_re * mix_im,
        ],
        1,
    )
    results = to_signal(prod_re, prod_im, frequencies, blocks, seq_index, seq_count, seq_count)
    convolved, carried, lag_grad = (results[0], results[1], results[2])
    skip_col = skip_gain[:, None, None]
    grad_query = (cot_f * (convolved + skip_col * mixed)).astype(jnp.bfloat16)
    grad_mixed = carried + skip_col * gated
    grad_key = (grad_mixed * value_f).astype(jnp.bfloat16)
    grad_value = (grad_mixed * key_f).astype(jnp.bfloat16)
    grad_filter = (lag_grad * norm_scale).astype(jnp.bfloat16)
    skip_part = jnp.sum(gated * mixed, axis=(1, 2))
    flat_shape = (chan_input, tok_local)
    grad_query = grad_query.reshape(flat_shape)
    grad_key = grad_key.reshape(flat_shape)
    grad_value = grad_value.reshape(flat_shape)
    grad_filter = grad_filter.reshape(flat_shape)
    skip_sum = lax.psum(skip_part, "seq")
    return (grad_query, grad_key, grad_value, grad_filter, skip_sum * norm_scale)


LANES = 128


def halves(table):
    high = table.astype(np.float32).astype(ml_dtypes.bfloat16)
    low = (table - high.astype(np.float64)).astype(np.float32).astype(ml_dtypes.bfloat16)
    return jnp.asarray(high), jnp.asarray(low)


def transform_tables(rows):
    total = rows * LANES
    quarter = np.arange(rows) + 0.25
    outer = 2.0 * np.pi / rows * np.outer(quarter, np.arange(rows))
    turn = 2.0 * np.pi / total * np.outer(quarter, np.arange(LANES))
    inner = 2.0 * np.pi / LANES * np.outer(np.arange(LANES), np.arange(LANES))
    first = np.concatenate([np.cos(outer), -np.sin(outer)], axis=0)
    second = np.block([[np.cos(inner), -np.sin(inner)], [np.sin(inner), np.cos(inner)]])
    second_back = np.block([[np.cos(inner), np.sin(inner)], [-np.sin(inner), np.cos(inner)]])
    first_back = np.concatenate([np.cos(outer.T), -np.sin(outer.T)], axis=1) / total
    return (
        *halves(first),
        *halves(second),
        *halves(second_back),
        *halves(first_back),
        jnp.asarray(np.cos(turn).astype(np.float32)),
        jnp.asarray(np.sin(turn).astype(np.float32)),
    )


def split(value):
    high = value.astype(jnp.bfloat16)
    low = (value - high.astype(jnp.float32)).astype(jnp.bfloat16)
    return high, low


def dot(left, right):
    return jnp.dot(left, right, preferred_element_type=jnp.float32)


def channel_kernel(
    count,
    query_ref, key_ref, value_ref, cot_ref, taps_ref, gain_ref,
    first_h, first_l, second_h, second_l, back2_h, back2_l, back1_h, back1_l, cos_ref, sin_ref,
    gq_ref, gk_ref, gv_ref, gf_ref, skip_ref,
    out_box, in_box, res_box, got_box, sum_box, sum_got,
    send_in, recv_in, send_res, recv_res, send_sum, recv_sum,
):
    me = lax.axis_index("seq")
    chans, tok_local = query_ref.shape
    per = chans // count
    part = tok_local // LANES
    rows = part * count
    norm_scale = 1.0 / math.sqrt(rows * LANES)

    def peer_of(step):
        return me ^ step

    barrier = pltpu.get_barrier_semaphore()
    for step in range(1, count):
        pl.semaphore_signal(barrier, inc=1, device_id={"seq": peer_of(step)}, device_id_type=pl.DeviceIdType.MESH)

    inputs = (query_ref, key_ref, value_ref, cot_ref, taps_ref)
    for slot, ref in enumerate(inputs):
        pieces = jnp.stack([ref[:, r * LANES : (r + 1) * LANES].astype(jnp.float32) for r in range(part)])
        turned = jnp.swapaxes(pieces, 0, 1).astype(jnp.bfloat16)
        out_box[:, :, slot] = turned.reshape(count, per, part, LANES)

    pl.semaphore_wait(barrier, count - 1)

    def send_copy(chan, step):
        peer = peer_of(step)
        return pltpu.make_async_remote_copy(
            src_ref=out_box.at[peer, chan],
            dst_ref=in_box.at[chan, me],
            send_sem=send_in.at[chan, step],
            recv_sem=recv_in.at[chan, step],
            device_id={"seq": peer},
            device_id_type=pl.DeviceIdType.MESH,
        )

    def result_copy(chan, step):
        peer = peer_of(step)
        return pltpu.make_async_remote_copy(
            src_ref=res_box.at[chan, peer],
            dst_ref=got_box.at[me, chan],
            send_sem=send_res.at[chan, step],
            recv_sem=recv_res.at[chan, step],
            device_id={"seq": peer},
            device_id_type=pl.DeviceIdType.MESH,
        )

    def sum_copy(step):
        peer = peer_of(step)
        return pltpu.make_async_remote_copy(
            src_ref=sum_box,
            dst_ref=sum_got.at[me],
            send_sem=send_sum.at[step],
            recv_sem=recv_sum.at[step],
            device_id={"seq": peer},
            device_id_type=pl.DeviceIdType.MESH,
        )

    for chan in range(per):
        for step in reversed(range(1, count)):
            send_copy(chan, step).start()
    for chan in range(per):
        in_box[chan, me] = out_box[me, chan]

    def one_channel(chan, carry):
        for step in range(1, count):
            send_copy(chan, step).wait_recv()
        arrived = [in_box[chan, :, slot].reshape(rows, LANES) for slot in range(5)]
        query_f, key_f, value_f, cot_f = [a.astype(jnp.float32) for a in arrived[:4]]
        taps = arrived[4]
        mixed = key_f * value_f
        gated = cot_f * query_f
        mixed_h, mixed_l = split(mixed)
        gated_h, gated_l = split(gated)

        high = jnp.concatenate([mixed_h, gated_h], axis=1)
        low = jnp.concatenate([mixed_l, gated_l], axis=1)
        pair = dot(first_h[...], high) + dot(first_h[...], low) + dot(first_l[...], high)
        both = dot(jnp.concatenate([first_h[...], first_l[...]], axis=0), taps)
        tap_out = both[: 2 * rows] + both[2 * rows :]
        cosine, sine = cos_ref[...], sin_ref[...]
        turned = []
        for block in (pair[:, :LANES], pair[:, LANES:], tap_out):
            real, imag = block[:rows], block[rows:]
            turned.append(jnp.concatenate([real * cosine + imag * sine, imag * cosine - real * sine], axis=1))
        work_h, work_l = split(jnp.concatenate(turned, axis=0))
        spec = dot(work_h, second_h[...]) + dot(work_l, second_h[...]) + dot(work_h, second_l[...])
        mix_re, mix_im = spec[:rows, :LANES], spec[:rows, LANES:]
        grad_re, grad_im = spec[rows : 2 * rows, :LANES], spec[rows : 2 * rows, LANES:]
        ker_re, ker_im = spec[2 * rows :, :LANES], spec[2 * rows :, LANES:]
        prods = jnp.concatenate(
            [
                jnp.concatenate([ker_re * mix_re - ker_im * mix_im, ker_re * mix_im + ker_im * mix_re], axis=1),
                jnp.concatenate([ker_re * grad_re + ker_im * grad_im, ker_re * grad_im - ker_im * grad_re], axis=1),
                jnp.concatenate([grad_re * mix_re + grad_im * mix_im, grad_im * mix_re - grad_re * mix_im], axis=1),
            ],
            axis=0,
        )
        prod_h, prod_l = split(prods)
        work = dot(prod_h, back2_h[...]) + dot(prod_l, back2_h[...]) + dot(prod_h, back2_l[...])
        turned = []
        for block in range(3):
            real = work[block * rows : (block + 1) * rows, :LANES]
            imag = work[block * rows : (block + 1) * rows, LANES:]
            turned.append(jnp.concatenate([real * cosine - imag * sine, imag * cosine + real * sine], axis=0))
        work_h, work_l = split(jnp.concatenate(turned, axis=1))
        result = dot(back1_h[...], work_h) + dot(back1_h[...], work_l) + dot(back1_l[...], work_h)
        convolved, carried, lag_grad = [result[:, i * LANES : (i + 1) * LANES] for i in range(3)]

        gain = gain_ref[me * per + chan]
        grad_mixed = carried + gain * gated
        finals = (
            cot_f * (convolved + gain * mixed),
            grad_mixed * value_f,
            grad_mixed * key_f,
            lag_grad * norm_scale,
        )
        for slot, value in enumerate(finals):
            res_box[chan, :, slot] = value.astype(jnp.bfloat16).reshape(count, part, LANES)
        for step in reversed(range(1, count)):
            result_copy(chan, step).start()
        total = jnp.sum(jnp.sum(gated * mixed, axis=0, keepdims=True), axis=1, keepdims=True) * norm_scale
        sum_box[chan] = jnp.broadcast_to(total, (8, LANES))
        return carry

    lax.fori_loop(0, per, one_channel, 0)

    for step in range(1, count):
        sum_copy(step).start()
    for chan in range(per):
        got_box[me, chan] = res_box[chan, me]
    sum_got[me] = sum_box[...]
    for chan in range(per):
        for step in range(1, count):
            send_copy(chan, step).wait_send()
    for step in range(1, count):
        sum_copy(step).wait()
    for chan in range(per):
        for step in range(1, count):
            result_copy(chan, step).wait()

    for slot, ref in enumerate((gq_ref, gk_ref, gv_ref, gf_ref)):
        pieces = got_box[:, :, slot].reshape(chans, part, LANES).astype(jnp.float32)
        turned = jnp.swapaxes(pieces, 0, 1).astype(jnp.bfloat16)
        for r in range(part):
            ref[:, r * LANES : (r + 1) * LANES] = turned[r]
    skip_ref[...] = sum_got[...].reshape(chans, 8, LANES)[:, 0, :]


def local_channels(queries, key_proj, value_proj, cotangent, filter_taps, skip_gain):
    count = lax.axis_size("seq")
    chans, tok_local = queries.shape
    per = chans // count
    part = tok_local // LANES
    rows = part * count
    tables = transform_tables(rows)
    vmem = pl.BlockSpec(memory_space=pltpu.VMEM)
    smem = pl.BlockSpec(memory_space=pltpu.SMEM)
    block = jax.ShapeDtypeStruct((chans, tok_local), jnp.bfloat16)
    dma = pltpu.SemaphoreType.DMA
    *grads, skips = pl.pallas_call(
        functools.partial(channel_kernel, count),
        out_shape=[block] * 4 + [jax.ShapeDtypeStruct((chans, LANES), jnp.float32)],
        in_specs=[vmem] * 5 + [smem] + [vmem] * 10,
        out_specs=[vmem] * 5,
        scratch_shapes=[
            pltpu.VMEM((count, per, 5, part, LANES), jnp.bfloat16),
            pltpu.VMEM((per, count, 5, part, LANES), jnp.bfloat16),
            pltpu.VMEM((per, count, 4, part, LANES), jnp.bfloat16),
            pltpu.VMEM((count, per, 4, part, LANES), jnp.bfloat16),
            pltpu.VMEM((per, 8, LANES), jnp.float32),
            pltpu.VMEM((count, per, 8, LANES), jnp.float32),
            dma((per, count)),
            dma((per, count)),
            dma((per, count)),
            dma((per, count)),
            dma((count,)),
            dma((count,)),
        ],
        compiler_params=pltpu.CompilerParams(
            collective_id=0, has_side_effects=True, vmem_limit_bytes=48 * 1024 * 1024
        ),
    )(queries, key_proj, value_proj, cotangent, filter_taps, skip_gain, *tables)
    return (*grads, skips[:, 0])


def local(*arguments):
    count = lax.axis_size("seq")
    chans, tok_local = arguments[0].shape
    whole_channels = chans % count == 0 and count & (count - 1) == 0
    if whole_channels and count > 1 and tok_local % (16 * LANES) == 0 and count * tok_local <= 65536:
        return local_channels(*arguments)
    return local_butterfly(*arguments)


def solution(mesh):
    return jax.shard_map(
        local,
        mesh=mesh,
        in_specs=(
            P("chan", "seq"),
            P("chan", "seq"),
            P("chan", "seq"),
            P("chan", "seq"),
            P("chan", "seq"),
            P("chan"),
        ),
        out_specs=(
            P("chan", "seq"),
            P("chan", "seq"),
            P("chan", "seq"),
            P("chan", "seq"),
            P("chan"),
        ),
        check_vma=False,
    )
```

```python
import functools
import math

import jax
import jax.numpy as jnp
import ml_dtypes
import numpy as np
from jax import lax
from jax.experimental import pallas as pl
from jax.experimental.pallas import tpu as pltpu
from jax.sharding import PartitionSpec as P

highest = lax.Precision.HIGHEST


def from_partner(block, axis, stride):
    count = lax.axis_size(axis)
    route = []
    for low in range(count):
        high = low | 1 << stride
        if high != low and high < count:
            route += [(low, high), (high, low)]
    return lax.ppermute(block, axis, route)


def complex_product(pattern, left_re, left_im, right_re, right_im):
    real_real = jnp.einsum(pattern, left_re, right_re, precision=highest)
    imag_imag = jnp.einsum(pattern, left_im, right_im, precision=highest)
    real_imag = jnp.einsum(pattern, left_re, right_im, precision=highest)
    imag_real = jnp.einsum(pattern, left_im, right_re, precision=highest)
    return (real_real - imag_imag, real_imag + imag_real)


def rotate(real_in, imag_in, angle_val):
    cosine = jnp.cos(angle_val)
    sine_val = jnp.sin(angle_val)
    return (real_in * cosine - imag_in * sine_val, real_in * sine_val + imag_in * cosine)


def dft_table(length, direction):
    counter = jnp.arange(length, dtype=jnp.int32)
    phase_idx = counter[:, None] * counter[None, :] % length
    angle_val = direction * 2.0 * math.pi / length * phase_idx.astype(jnp.float32)
    return (jnp.cos(angle_val), jnp.sin(angle_val))


def twiddle_angle(row_count, radix_len, length, direction):
    phase_idx = (
        jnp.arange(row_count, dtype=jnp.int32)[:, None]
        * jnp.arange(radix_len, dtype=jnp.int32)[None, :]
        % length
    )
    return direction * 2.0 * math.pi / length * phase_idx.astype(jnp.float32)


def local_forward(real_in, imag_in):
    length = real_in.shape[-1]
    radix_len = math.gcd(length, 512)
    row_count = length // radix_len
    new_shape = real_in.shape[:-1] + (row_count, radix_len)
    first_re, first_im = dft_table(row_count, -1.0)
    work_re, work_im = complex_product(
        "ab,...bj->...aj",
        first_re,
        first_im,
        real_in.reshape(new_shape),
        imag_in.reshape(new_shape),
    )
    work_re, work_im = rotate(work_re, work_im, twiddle_angle(row_count, radix_len, length, -1.0))
    second_re, second_im = dft_table(radix_len, -1.0)
    work_re, work_im = complex_product("...aj,jk->...ak", work_re, work_im, second_re, second_im)
    return (work_re.reshape(real_in.shape), work_im.reshape(real_in.shape))


def local_inverse(real_in, imag_in):
    length = real_in.shape[-1]
    radix_len = math.gcd(length, 512)
    row_count = length // radix_len
    new_shape = real_in.shape[:-1] + (row_count, radix_len)
    second_re, second_im = dft_table(radix_len, 1.0)
    work_re, work_im = complex_product(
        "...ak,kj->...aj",
        real_in.reshape(new_shape),
        imag_in.reshape(new_shape),
        second_re,
        second_im,
    )
    work_re, work_im = rotate(work_re, work_im, twiddle_angle(row_count, radix_len, length, 1.0))
    first_re, first_im = dft_table(row_count, 1.0)
    work_re, work_im = complex_product("ab,...aj->...bj", first_re, first_im, work_re, work_im)
    return (work_re.reshape(real_in.shape), work_im.reshape(real_in.shape))


def bit_reverse(seq_index, bit_total):
    reversed_idx = jnp.zeros_like(seq_index)
    for bit_level in range(bit_total):
        reversed_idx = reversed_idx | (seq_index >> bit_level & 1) << bit_total - 1 - bit_level
    return reversed_idx


def frequency_angle(frequencies, lane_count, padded_len, direction):
    lanes = jnp.arange(lane_count, dtype=jnp.int32)
    parity = jnp.arange(2, dtype=jnp.int32)
    spectral = 2 * frequencies[None, :] + parity[:, None]
    phase_idx = spectral[:, :, None] * lanes[None, None, :] % padded_len
    angle_val = direction * 2.0 * math.pi / padded_len * phase_idx.astype(jnp.float32)
    return angle_val[:, None, None]


def to_spectrum(signals, blocks, seq_index, seq_count, block_total):
    lane_count = signals.shape[-1]
    padded_len = 2 * block_total * lane_count
    half_turn = (math.pi / block_total * blocks.astype(jnp.float32))[:, None]
    real_part = jnp.stack([signals, signals * jnp.cos(half_turn)])
    imag_part = jnp.stack([jnp.zeros_like(signals), -signals * jnp.sin(half_turn)])
    bit_total = seq_count.bit_length() - 1
    for bit_level in reversed(range(bit_total)):
        half_span = 1 << bit_level
        other_re, other_im = from_partner((real_part, imag_part), "seq", bit_level)
        position = seq_index % (2 * half_span)
        is_upper = position < half_span
        sum_re = jnp.where(is_upper, real_part + other_re, other_re - real_part)
        sum_im = jnp.where(is_upper, imag_part + other_im, other_im - imag_part)
        angle_val = jnp.where(
            is_upper, 0.0, -math.pi * (position % half_span).astype(jnp.float32) / half_span
        )
        real_part, imag_part = rotate(sum_re, sum_im, angle_val)
    frequencies = bit_reverse(seq_index, bit_total)[None]
    real_part, imag_part = rotate(
        real_part, imag_part, frequency_angle(frequencies, lane_count, padded_len, -1.0)
    )
    return (local_forward(real_part, imag_part), frequencies)


def to_signal(real_part, imag_part, frequencies, blocks, seq_index, seq_count, block_total):
    lane_count = real_part.shape[-1]
    padded_len = 2 * block_total * lane_count
    real_part, imag_part = local_inverse(real_part, imag_part)
    real_part, imag_part = rotate(
        real_part, imag_part, frequency_angle(frequencies, lane_count, padded_len, 1.0)
    )
    bit_total = seq_count.bit_length() - 1
    for bit_level in range(bit_total):
        half_span = 1 << bit_level
        other_re, other_im = from_partner((real_part, imag_part), "seq", bit_level)
        position = seq_index % (2 * half_span)
        is_upper = position < half_span
        taken_re = jnp.where(is_upper, other_re, real_part)
        taken_im = jnp.where(is_upper, other_im, imag_part)
        base_re = jnp.where(is_upper, real_part, other_re)
        base_im = jnp.where(is_upper, imag_part, other_im)
        angle_val = math.pi * (position % half_span).astype(jnp.float32) / half_span
        turned_re, turned_im = rotate(taken_re, taken_im, angle_val)
        flip_sign = jnp.where(is_upper, 1.0, -1.0)
        real_part = base_re + flip_sign * turned_re
        imag_part = base_im + flip_sign * turned_im
    half_turn = (math.pi / block_total * blocks.astype(jnp.float32))[:, None]
    combined = real_part[0] + real_part[1] * jnp.cos(half_turn) - imag_part[1] * jnp.sin(half_turn)
    return combined / padded_len


def local_butterfly(queries, key_proj, value_proj, cotangent, filter_taps, skip_gain):
    seq_count = lax.axis_size("seq")
    seq_index = lax.axis_index("seq")
    tok_local = queries.shape[1]
    tokens_all = seq_count * tok_local
    norm_scale = 1.0 / math.sqrt(tokens_all)
    chan_input = queries.shape[0]
    query_in, key_in, value_in, cot_in, taps_in = (
        queries,
        key_proj,
        value_proj,
        cotangent,
        filter_taps,
    )
    blocks = seq_index[None]
    block_shape = (chan_input, blocks.shape[0], tok_local)
    query_f = query_in.reshape(block_shape).astype(jnp.float32)
    key_f = key_in.reshape(block_shape).astype(jnp.float32)
    value_f = value_in.reshape(block_shape).astype(jnp.float32)
    cot_f = cot_in.reshape(block_shape).astype(jnp.float32)
    kernel = taps_in.reshape(block_shape).astype(jnp.float32)
    mixed = key_f * value_f
    gated = cot_f * query_f
    signals = jnp.stack([mixed, gated, kernel])
    (spec_re, spec_im), frequencies = to_spectrum(signals, blocks, seq_index, seq_count, seq_count)
    mix_re, mix_im = (spec_re[:, 0], spec_im[:, 0])
    grad_re, grad_im = (spec_re[:, 1], spec_im[:, 1])
    ker_re, ker_im = (spec_re[:, 2], spec_im[:, 2])
    prod_re = jnp.stack(
        [
            ker_re * mix_re - ker_im * mix_im,
            ker_re * grad_re + ker_im * grad_im,
            grad_re * mix_re + grad_im * mix_im,
        ],
        1,
    )
    prod_im = jnp.stack(
        [
            ker_re * mix_im + ker_im * mix_re,
            ker_re * grad_im - ker_im * grad_re,
            grad_im * mix_re - grad_re * mix_im,
        ],
        1,
    )
    results = to_signal(prod_re, prod_im, frequencies, blocks, seq_index, seq_count, seq_count)
    convolved, carried, lag_grad = (results[0], results[1], results[2])
    skip_col = skip_gain[:, None, None]
    grad_query = (cot_f * (convolved + skip_col * mixed)).astype(jnp.bfloat16)
    grad_mixed = carried + skip_col * gated
    grad_key = (grad_mixed * value_f).astype(jnp.bfloat16)
    grad_value = (grad_mixed * key_f).astype(jnp.bfloat16)
    grad_filter = (lag_grad * norm_scale).astype(jnp.bfloat16)
    skip_part = jnp.sum(gated * mixed, axis=(1, 2))
    flat_shape = (chan_input, tok_local)
    grad_query = grad_query.reshape(flat_shape)
    grad_key = grad_key.reshape(flat_shape)
    grad_value = grad_value.reshape(flat_shape)
    grad_filter = grad_filter.reshape(flat_shape)
    skip_sum = lax.psum(skip_part, "seq")
    return (grad_query, grad_key, grad_value, grad_filter, skip_sum * norm_scale)


LANES = 128


def halves(table):
    high = table.astype(np.float32).astype(ml_dtypes.bfloat16)
    low = (table - high.astype(np.float64)).astype(np.float32).astype(ml_dtypes.bfloat16)
    return jnp.asarray(high), jnp.asarray(low)


def transform_tables(rows):
    total = rows * LANES
    quarter = np.arange(rows) + 0.25
    outer = 2.0 * np.pi / rows * np.outer(quarter, np.arange(rows))
    turn = 2.0 * np.pi / total * np.outer(quarter, np.arange(LANES))
    inner = 2.0 * np.pi / LANES * np.outer(np.arange(LANES), np.arange(LANES))
    first = np.concatenate([np.cos(outer), -np.sin(outer)], axis=0)
    second = np.block([[np.cos(inner), -np.sin(inner)], [np.sin(inner), np.cos(inner)]])
    second_back = np.block([[np.cos(inner), np.sin(inner)], [-np.sin(inner), np.cos(inner)]])
    first_back = np.concatenate([np.cos(outer.T), -np.sin(outer.T)], axis=1) / total
    return (
        *halves(first),
        *halves(second),
        *halves(second_back),
        *halves(first_back),
        jnp.asarray(np.cos(turn).astype(np.float32)),
        jnp.asarray(np.sin(turn).astype(np.float32)),
    )


def split(value):
    high = value.astype(jnp.bfloat16)
    low = (value - high.astype(jnp.float32)).astype(jnp.bfloat16)
    return high, low


def dot(left, right):
    return jnp.dot(left, right, preferred_element_type=jnp.float32)


def channel_kernel(
    count,
    *refs,
):
    args, gain_ref, tables, refs = refs[:5], refs[5], refs[6:16], refs[16:]
    gq_ref, gk_ref, gv_ref, gf_ref, skip_ref = refs[:5]
    arg_vmem, table_vmem, refs = refs[5:10], refs[10:20], refs[20:]
    out_box, in_box, res_box, got_box, sum_box, sum_got = refs[:6]
    send_in, recv_in, send_res, recv_res, send_sum, recv_sum, load_sem = refs[6:]
    first_h, first_l, second_h, second_l, back2_h, back2_l, back1_h, back1_l, cos_ref, sin_ref = table_vmem
    me = lax.axis_index("seq")
    chans, tok_local = args[0].shape
    per = chans // count
    part = tok_local // LANES
    rows = part * count
    norm_scale = 1.0 / math.sqrt(rows * LANES)

    loads = [
        pltpu.make_async_copy(source, target, load_sem.at[i])
        for i, (source, target) in enumerate(zip(args + tables, arg_vmem + table_vmem))
    ]
    for load in loads[:5]:
        load.start()

    def peer_of(step):
        return me ^ step

    barrier = pltpu.get_barrier_semaphore()
    for step in range(1, count):
        pl.semaphore_signal(barrier, inc=1, device_id={"seq": peer_of(step)}, device_id_type=pl.DeviceIdType.MESH)

    for load in loads[5:]:
        load.start()
    for slot, ref in enumerate(arg_vmem):
        loads[slot].wait()
        pieces = jnp.stack([ref[:, r * LANES : (r + 1) * LANES].astype(jnp.float32) for r in range(part)])
        turned = jnp.swapaxes(pieces, 0, 1).astype(jnp.bfloat16)
        out_box[:, :, slot] = turned.reshape(count, per, part, LANES)

    pl.semaphore_wait(barrier, count - 1)

    def send_copy(chan, step):
        peer = peer_of(step)
        return pltpu.make_async_remote_copy(
            src_ref=out_box.at[peer, chan],
            dst_ref=in_box.at[chan, me],
            send_sem=send_in.at[chan, step],
            recv_sem=recv_in.at[chan, step],
            device_id={"seq": peer},
            device_id_type=pl.DeviceIdType.MESH,
        )

    def result_copy(chan, step):
        peer = peer_of(step)
        return pltpu.make_async_remote_copy(
            src_ref=res_box.at[chan, peer],
            dst_ref=got_box.at[me, chan],
            send_sem=send_res.at[chan, step],
            recv_sem=recv_res.at[chan, step],
            device_id={"seq": peer},
            device_id_type=pl.DeviceIdType.MESH,
        )

    def sum_copy(step):
        peer = peer_of(step)
        return pltpu.make_async_remote_copy(
            src_ref=sum_box,
            dst_ref=sum_got.at[me],
            send_sem=send_sum.at[step],
            recv_sem=recv_sum.at[step],
            device_id={"seq": peer},
            device_id_type=pl.DeviceIdType.MESH,
        )

    for chan in range(per):
        for step in reversed(range(1, count)):
            send_copy(chan, step).start()
    for chan in range(per):
        in_box[chan, me] = out_box[me, chan]

    for load in loads[5:]:
        load.wait()

    def one_channel(chan, carry):
        for step in range(1, count):
            send_copy(chan, step).wait_recv()
        arrived = [in_box[chan, :, slot].reshape(rows, LANES) for slot in range(5)]
        query_f, key_f, value_f, cot_f = [a.astype(jnp.float32) for a in arrived[:4]]
        taps = arrived[4]
        mixed = key_f * value_f
        gated = cot_f * query_f
        mixed_h, mixed_l = split(mixed)
        gated_h, gated_l = split(gated)

        high = jnp.concatenate([mixed_h, gated_h], axis=1)
        low = jnp.concatenate([mixed_l, gated_l], axis=1)
        pair = dot(first_h[...], high) + dot(first_h[...], low) + dot(first_l[...], high)
        both = dot(jnp.concatenate([first_h[...], first_l[...]], axis=0), taps)
        tap_out = both[: 2 * rows] + both[2 * rows :]
        cosine, sine = cos_ref[...], sin_ref[...]
        turned = []
        for block in (pair[:, :LANES], pair[:, LANES:], tap_out):
            real, imag = block[:rows], block[rows:]
            turned.append(jnp.concatenate([real * cosine + imag * sine, imag * cosine - real * sine], axis=1))
        work_h, work_l = split(jnp.concatenate(turned, axis=0))
        spec = dot(work_h, second_h[...]) + dot(work_l, second_h[...]) + dot(work_h, second_l[...])
        mix_re, mix_im = spec[:rows, :LANES], spec[:rows, LANES:]
        grad_re, grad_im = spec[rows : 2 * rows, :LANES], spec[rows : 2 * rows, LANES:]
        ker_re, ker_im = spec[2 * rows :, :LANES], spec[2 * rows :, LANES:]
        prods = jnp.concatenate(
            [
                jnp.concatenate([ker_re * mix_re - ker_im * mix_im, ker_re * mix_im + ker_im * mix_re], axis=1),
                jnp.concatenate([ker_re * grad_re + ker_im * grad_im, ker_re * grad_im - ker_im * grad_re], axis=1),
                jnp.concatenate([grad_re * mix_re + grad_im * mix_im, grad_im * mix_re - grad_re * mix_im], axis=1),
            ],
            axis=0,
        )
        prod_h, prod_l = split(prods)
        work = dot(prod_h, back2_h[...]) + dot(prod_l, back2_h[...]) + dot(prod_h, back2_l[...])
        turned = []
        for block in range(3):
            real = work[block * rows : (block + 1) * rows, :LANES]
            imag = work[block * rows : (block + 1) * rows, LANES:]
            turned.append(jnp.concatenate([real * cosine - imag * sine, imag * cosine + real * sine], axis=0))
        work_h, work_l = split(jnp.concatenate(turned, axis=1))
        result = dot(back1_h[...], work_h) + dot(back1_h[...], work_l) + dot(back1_l[...], work_h)
        convolved, carried, lag_grad = [result[:, i * LANES : (i + 1) * LANES] for i in range(3)]

        gain = gain_ref[me * per + chan]
        grad_mixed = carried + gain * gated
        finals = (
            cot_f * (convolved + gain * mixed),
            grad_mixed * value_f,
            grad_mixed * key_f,
            lag_grad * norm_scale,
        )
        for slot, value in enumerate(finals):
            res_box[chan, :, slot] = value.astype(jnp.bfloat16).reshape(count, part, LANES)
        for step in reversed(range(1, count)):
            result_copy(chan, step).start()
        total = jnp.sum(jnp.sum(gated * mixed, axis=0, keepdims=True), axis=1, keepdims=True) * norm_scale
        sum_box[chan] = jnp.broadcast_to(total, (8, LANES))
        return carry

    lax.fori_loop(0, per, one_channel, 0)

    for step in range(1, count):
        sum_copy(step).start()
    for chan in range(per):
        got_box[me, chan] = res_box[chan, me]
    sum_got[me] = sum_box[...]
    for chan in range(per):
        for step in range(1, count):
            send_copy(chan, step).wait_send()
    for step in range(1, count):
        sum_copy(step).wait()
    for chan in range(per):
        for step in range(1, count):
            result_copy(chan, step).wait()

    for slot, ref in enumerate((gq_ref, gk_ref, gv_ref, gf_ref)):
        pieces = got_box[:, :, slot].reshape(chans, part, LANES).astype(jnp.float32)
        turned = jnp.swapaxes(pieces, 0, 1).astype(jnp.bfloat16)
        for r in range(part):
            ref[:, r * LANES : (r + 1) * LANES] = turned[r]
    skip_ref[...] = sum_got[...].reshape(chans, 8, LANES)[:, 0, :]


def local_channels(queries, key_proj, value_proj, cotangent, filter_taps, skip_gain):
    count = lax.axis_size("seq")
    chans, tok_local = queries.shape
    per = chans // count
    part = tok_local // LANES
    rows = part * count
    tables = transform_tables(rows)
    vmem = pl.BlockSpec(memory_space=pltpu.VMEM)
    hbm = pl.BlockSpec(memory_space=pltpu.HBM)
    smem = pl.BlockSpec(memory_space=pltpu.SMEM)
    block = jax.ShapeDtypeStruct((chans, tok_local), jnp.bfloat16)
    dma = pltpu.SemaphoreType.DMA
    *grads, skips = pl.pallas_call(
        functools.partial(channel_kernel, count),
        out_shape=[block] * 4 + [jax.ShapeDtypeStruct((chans, LANES), jnp.float32)],
        in_specs=[hbm] * 5 + [smem] + [hbm] * 10,
        out_specs=[vmem] * 5,
        scratch_shapes=[
            *[pltpu.VMEM((chans, tok_local), jnp.bfloat16) for _ in range(5)],
            *[pltpu.VMEM(table.shape, table.dtype) for table in tables],
            pltpu.VMEM((count, per, 5, part, LANES), jnp.bfloat16),
            pltpu.VMEM((per, count, 5, part, LANES), jnp.bfloat16),
            pltpu.VMEM((per, count, 4, part, LANES), jnp.bfloat16),
            pltpu.VMEM((count, per, 4, part, LANES), jnp.bfloat16),
            pltpu.VMEM((per, 8, LANES), jnp.float32),
            pltpu.VMEM((count, per, 8, LANES), jnp.float32),
            dma((per, count)),
            dma((per, count)),
            dma((per, count)),
            dma((per, count)),
            dma((count,)),
            dma((count,)),
            dma((15,)),
        ],
        compiler_params=pltpu.CompilerParams(
            collective_id=0, has_side_effects=True, vmem_limit_bytes=48 * 1024 * 1024
        ),
    )(queries, key_proj, value_proj, cotangent, filter_taps, skip_gain, *tables)
    return (*grads, skips[:, 0])


def local(*arguments):
    count = lax.axis_size("seq")
    chans, tok_local = arguments[0].shape
    whole_channels = chans % count == 0 and count & (count - 1) == 0
    if whole_channels and count > 1 and tok_local % (16 * LANES) == 0 and count * tok_local <= 65536:
        return local_channels(*arguments)
    return local_butterfly(*arguments)


def solution(mesh):
    return jax.shard_map(
        local,
        mesh=mesh,
        in_specs=(
            P("chan", "seq"),
            P("chan", "seq"),
            P("chan", "seq"),
            P("chan", "seq"),
            P("chan", "seq"),
            P("chan"),
        ),
        out_specs=(
            P("chan", "seq"),
            P("chan", "seq"),
            P("chan", "seq"),
            P("chan", "seq"),
            P("chan"),
        ),
        check_vma=False,
    )
```

```python
import functools
import math

import jax
import jax.numpy as jnp
import ml_dtypes
import numpy as np
from jax import lax
from jax.experimental import pallas as pl
from jax.experimental.pallas import tpu as pltpu
from jax.sharding import PartitionSpec as P

highest = lax.Precision.HIGHEST


def from_partner(block, axis, stride):
    count = lax.axis_size(axis)
    route = []
    for low in range(count):
        high = low | 1 << stride
        if high != low and high < count:
            route += [(low, high), (high, low)]
    return lax.ppermute(block, axis, route)


def complex_product(pattern, left_re, left_im, right_re, right_im):
    real_real = jnp.einsum(pattern, left_re, right_re, precision=highest)
    imag_imag = jnp.einsum(pattern, left_im, right_im, precision=highest)
    real_imag = jnp.einsum(pattern, left_re, right_im, precision=highest)
    imag_real = jnp.einsum(pattern, left_im, right_re, precision=highest)
    return (real_real - imag_imag, real_imag + imag_real)


def rotate(real_in, imag_in, angle_val):
    cosine = jnp.cos(angle_val)
    sine_val = jnp.sin(angle_val)
    return (real_in * cosine - imag_in * sine_val, real_in * sine_val + imag_in * cosine)


def dft_table(length, direction):
    counter = jnp.arange(length, dtype=jnp.int32)
    phase_idx = counter[:, None] * counter[None, :] % length
    angle_val = direction * 2.0 * math.pi / length * phase_idx.astype(jnp.float32)
    return (jnp.cos(angle_val), jnp.sin(angle_val))


def twiddle_angle(row_count, radix_len, length, direction):
    phase_idx = (
        jnp.arange(row_count, dtype=jnp.int32)[:, None]
        * jnp.arange(radix_len, dtype=jnp.int32)[None, :]
        % length
    )
    return direction * 2.0 * math.pi / length * phase_idx.astype(jnp.float32)


def local_forward(real_in, imag_in):
    length = real_in.shape[-1]
    radix_len = math.gcd(length, 512)
    row_count = length // radix_len
    new_shape = real_in.shape[:-1] + (row_count, radix_len)
    first_re, first_im = dft_table(row_count, -1.0)
    work_re, work_im = complex_product(
        "ab,...bj->...aj",
        first_re,
        first_im,
        real_in.reshape(new_shape),
        imag_in.reshape(new_shape),
    )
    work_re, work_im = rotate(work_re, work_im, twiddle_angle(row_count, radix_len, length, -1.0))
    second_re, second_im = dft_table(radix_len, -1.0)
    work_re, work_im = complex_product("...aj,jk->...ak", work_re, work_im, second_re, second_im)
    return (work_re.reshape(real_in.shape), work_im.reshape(real_in.shape))


def local_inverse(real_in, imag_in):
    length = real_in.shape[-1]
    radix_len = math.gcd(length, 512)
    row_count = length // radix_len
    new_shape = real_in.shape[:-1] + (row_count, radix_len)
    second_re, second_im = dft_table(radix_len, 1.0)
    work_re, work_im = complex_product(
        "...ak,kj->...aj",
        real_in.reshape(new_shape),
        imag_in.reshape(new_shape),
        second_re,
        second_im,
    )
    work_re, work_im = rotate(work_re, work_im, twiddle_angle(row_count, radix_len, length, 1.0))
    first_re, first_im = dft_table(row_count, 1.0)
    work_re, work_im = complex_product("ab,...aj->...bj", first_re, first_im, work_re, work_im)
    return (work_re.reshape(real_in.shape), work_im.reshape(real_in.shape))


def bit_reverse(seq_index, bit_total):
    reversed_idx = jnp.zeros_like(seq_index)
    for bit_level in range(bit_total):
        reversed_idx = reversed_idx | (seq_index >> bit_level & 1) << bit_total - 1 - bit_level
    return reversed_idx


def frequency_angle(frequencies, lane_count, padded_len, direction):
    lanes = jnp.arange(lane_count, dtype=jnp.int32)
    parity = jnp.arange(2, dtype=jnp.int32)
    spectral = 2 * frequencies[None, :] + parity[:, None]
    phase_idx = spectral[:, :, None] * lanes[None, None, :] % padded_len
    angle_val = direction * 2.0 * math.pi / padded_len * phase_idx.astype(jnp.float32)
    return angle_val[:, None, None]


def to_spectrum(signals, blocks, seq_index, seq_count, block_total):
    lane_count = signals.shape[-1]
    padded_len = 2 * block_total * lane_count
    half_turn = (math.pi / block_total * blocks.astype(jnp.float32))[:, None]
    real_part = jnp.stack([signals, signals * jnp.cos(half_turn)])
    imag_part = jnp.stack([jnp.zeros_like(signals), -signals * jnp.sin(half_turn)])
    bit_total = seq_count.bit_length() - 1
    for bit_level in reversed(range(bit_total)):
        half_span = 1 << bit_level
        other_re, other_im = from_partner((real_part, imag_part), "seq", bit_level)
        position = seq_index % (2 * half_span)
        is_upper = position < half_span
        sum_re = jnp.where(is_upper, real_part + other_re, other_re - real_part)
        sum_im = jnp.where(is_upper, imag_part + other_im, other_im - imag_part)
        angle_val = jnp.where(
            is_upper, 0.0, -math.pi * (position % half_span).astype(jnp.float32) / half_span
        )
        real_part, imag_part = rotate(sum_re, sum_im, angle_val)
    frequencies = bit_reverse(seq_index, bit_total)[None]
    real_part, imag_part = rotate(
        real_part, imag_part, frequency_angle(frequencies, lane_count, padded_len, -1.0)
    )
    return (local_forward(real_part, imag_part), frequencies)


def to_signal(real_part, imag_part, frequencies, blocks, seq_index, seq_count, block_total):
    lane_count = real_part.shape[-1]
    padded_len = 2 * block_total * lane_count
    real_part, imag_part = local_inverse(real_part, imag_part)
    real_part, imag_part = rotate(
        real_part, imag_part, frequency_angle(frequencies, lane_count, padded_len, 1.0)
    )
    bit_total = seq_count.bit_length() - 1
    for bit_level in range(bit_total):
        half_span = 1 << bit_level
        other_re, other_im = from_partner((real_part, imag_part), "seq", bit_level)
        position = seq_index % (2 * half_span)
        is_upper = position < half_span
        taken_re = jnp.where(is_upper, other_re, real_part)
        taken_im = jnp.where(is_upper, other_im, imag_part)
        base_re = jnp.where(is_upper, real_part, other_re)
        base_im = jnp.where(is_upper, imag_part, other_im)
        angle_val = math.pi * (position % half_span).astype(jnp.float32) / half_span
        turned_re, turned_im = rotate(taken_re, taken_im, angle_val)
        flip_sign = jnp.where(is_upper, 1.0, -1.0)
        real_part = base_re + flip_sign * turned_re
        imag_part = base_im + flip_sign * turned_im
    half_turn = (math.pi / block_total * blocks.astype(jnp.float32))[:, None]
    combined = real_part[0] + real_part[1] * jnp.cos(half_turn) - imag_part[1] * jnp.sin(half_turn)
    return combined / padded_len


def local_butterfly(queries, key_proj, value_proj, cotangent, filter_taps, skip_gain):
    seq_count = lax.axis_size("seq")
    seq_index = lax.axis_index("seq")
    tok_local = queries.shape[1]
    tokens_all = seq_count * tok_local
    norm_scale = 1.0 / math.sqrt(tokens_all)
    chan_input = queries.shape[0]
    query_in, key_in, value_in, cot_in, taps_in = (
        queries,
        key_proj,
        value_proj,
        cotangent,
        filter_taps,
    )
    blocks = seq_index[None]
    block_shape = (chan_input, blocks.shape[0], tok_local)
    query_f = query_in.reshape(block_shape).astype(jnp.float32)
    key_f = key_in.reshape(block_shape).astype(jnp.float32)
    value_f = value_in.reshape(block_shape).astype(jnp.float32)
    cot_f = cot_in.reshape(block_shape).astype(jnp.float32)
    kernel = taps_in.reshape(block_shape).astype(jnp.float32)
    mixed = key_f * value_f
    gated = cot_f * query_f
    signals = jnp.stack([mixed, gated, kernel])
    (spec_re, spec_im), frequencies = to_spectrum(signals, blocks, seq_index, seq_count, seq_count)
    mix_re, mix_im = (spec_re[:, 0], spec_im[:, 0])
    grad_re, grad_im = (spec_re[:, 1], spec_im[:, 1])
    ker_re, ker_im = (spec_re[:, 2], spec_im[:, 2])
    prod_re = jnp.stack(
        [
            ker_re * mix_re - ker_im * mix_im,
            ker_re * grad_re + ker_im * grad_im,
            grad_re * mix_re + grad_im * mix_im,
        ],
        1,
    )
    prod_im = jnp.stack(
        [
            ker_re * mix_im + ker_im * mix_re,
            ker_re * grad_im - ker_im * grad_re,
            grad_im * mix_re - grad_re * mix_im,
        ],
        1,
    )
    results = to_signal(prod_re, prod_im, frequencies, blocks, seq_index, seq_count, seq_count)
    convolved, carried, lag_grad = (results[0], results[1], results[2])
    skip_col = skip_gain[:, None, None]
    grad_query = (cot_f * (convolved + skip_col * mixed)).astype(jnp.bfloat16)
    grad_mixed = carried + skip_col * gated
    grad_key = (grad_mixed * value_f).astype(jnp.bfloat16)
    grad_value = (grad_mixed * key_f).astype(jnp.bfloat16)
    grad_filter = (lag_grad * norm_scale).astype(jnp.bfloat16)
    skip_part = jnp.sum(gated * mixed, axis=(1, 2))
    flat_shape = (chan_input, tok_local)
    grad_query = grad_query.reshape(flat_shape)
    grad_key = grad_key.reshape(flat_shape)
    grad_value = grad_value.reshape(flat_shape)
    grad_filter = grad_filter.reshape(flat_shape)
    skip_sum = lax.psum(skip_part, "seq")
    return (grad_query, grad_key, grad_value, grad_filter, skip_sum * norm_scale)


LANES = 128


def halves(table):
    high = table.astype(np.float32).astype(ml_dtypes.bfloat16)
    low = (table - high.astype(np.float64)).astype(np.float32).astype(ml_dtypes.bfloat16)
    return high, low


def transform_tables(rows):
    total = rows * LANES
    quarter = np.arange(rows) + 0.25
    outer = 2.0 * np.pi / rows * np.outer(quarter, np.arange(rows))
    turn = 2.0 * np.pi / total * np.outer(quarter, np.arange(LANES))
    inner = 2.0 * np.pi / LANES * np.outer(np.arange(LANES), np.arange(LANES))
    first = np.concatenate([np.cos(outer), -np.sin(outer)], axis=0)
    second = np.block([[np.cos(inner), -np.sin(inner)], [np.sin(inner), np.cos(inner)]])
    second_back = np.block([[np.cos(inner), np.sin(inner)], [-np.sin(inner), np.cos(inner)]])
    first_back = np.concatenate([np.cos(outer.T), -np.sin(outer.T)], axis=1) / total
    parts = halves(first) + halves(second) + halves(second_back)
    for table in halves(first_back):
        parts += (table[:, :rows], table[:, rows:])
    turns = np.concatenate([np.cos(turn), np.sin(turn)]).astype(np.float32)
    return jnp.asarray(np.concatenate(parts)), jnp.asarray(turns)


def split(value):
    high = value.astype(jnp.bfloat16)
    low = (value - high.astype(jnp.float32)).astype(jnp.bfloat16)
    return high, low


def dot(left, right):
    return jnp.dot(left, right, preferred_element_type=jnp.float32)


def channel_kernel(
    count,
    *refs,
):
    args, gain_ref, tables, refs = refs[:5], refs[5], refs[6:8], refs[8:]
    gq_ref, gk_ref, gv_ref, gf_ref, skip_ref = refs[:5]
    arg_vmem, table_vmem, refs = refs[5:10], refs[10:12], refs[12:]
    out_box, in_box, res_box, got_box, sum_box, sum_got = refs[:6]
    send_in, recv_in, send_res, recv_res, send_sum, recv_sum, load_sem = refs[6:]
    table_ref, turn_ref = table_vmem
    me = lax.axis_index("seq")
    chans, tok_local = args[0].shape
    per = chans // count
    part = tok_local // LANES
    rows = part * count
    norm_scale = 1.0 / math.sqrt(rows * LANES)

    loads = [
        pltpu.make_async_copy(source, target, load_sem.at[i])
        for i, (source, target) in enumerate(zip(args + tables, arg_vmem + table_vmem))
    ]
    for load in loads[:5]:
        load.start()

    def peer_of(step):
        return me ^ step

    barrier = pltpu.get_barrier_semaphore()
    for step in range(1, count):
        pl.semaphore_signal(barrier, inc=1, device_id={"seq": peer_of(step)}, device_id_type=pl.DeviceIdType.MESH)

    for load in loads[5:]:
        load.start()
    for slot, ref in enumerate(arg_vmem):
        loads[slot].wait()
        pieces = jnp.stack([ref[:, r * LANES : (r + 1) * LANES].astype(jnp.float32) for r in range(part)])
        turned = jnp.swapaxes(pieces, 0, 1).astype(jnp.bfloat16)
        out_box[:, :, slot] = turned.reshape(count, per, part, LANES)

    pl.semaphore_wait(barrier, count - 1)

    def send_copy(chan, step):
        peer = peer_of(step)
        return pltpu.make_async_remote_copy(
            src_ref=out_box.at[peer, chan],
            dst_ref=in_box.at[chan, me],
            send_sem=send_in.at[chan, step],
            recv_sem=recv_in.at[chan, step],
            device_id={"seq": peer},
            device_id_type=pl.DeviceIdType.MESH,
        )

    def result_copy(chan, step):
        peer = peer_of(step)
        return pltpu.make_async_remote_copy(
            src_ref=res_box.at[chan, peer],
            dst_ref=got_box.at[me, chan],
            send_sem=send_res.at[chan, step],
            recv_sem=recv_res.at[chan, step],
            device_id={"seq": peer},
            device_id_type=pl.DeviceIdType.MESH,
        )

    def sum_copy(step):
        peer = peer_of(step)
        return pltpu.make_async_remote_copy(
            src_ref=sum_box,
            dst_ref=sum_got.at[me],
            send_sem=send_sum.at[step],
            recv_sem=recv_sum.at[step],
            device_id={"seq": peer},
            device_id_type=pl.DeviceIdType.MESH,
        )

    for chan in range(per):
        for step in reversed(range(1, count)):
            send_copy(chan, step).start()
    for chan in range(per):
        in_box[chan, me] = out_box[me, chan]

    for load in loads[5:]:
        load.wait()

    def table(first, blocks=1):
        return table_ref[first * rows : (first + blocks) * rows]

    def one_channel(chan, carry):
        for step in range(1, count):
            send_copy(chan, step).wait_recv()
        arrived = [in_box[chan, :, slot].reshape(rows, LANES) for slot in range(5)]
        query_f, key_f, value_f, cot_f = [a.astype(jnp.float32) for a in arrived[:4]]
        taps = arrived[4]
        mixed = key_f * value_f
        gated = cot_f * query_f
        mixed_h, mixed_l = split(mixed)
        gated_h, gated_l = split(gated)

        high = jnp.concatenate([mixed_h, gated_h], axis=1)
        low = jnp.concatenate([mixed_l, gated_l], axis=1)
        pair = dot(table(0, 2), high) + dot(table(0, 2), low) + dot(table(2, 2), high)
        both = dot(table(0, 4), taps)
        tap_out = both[: 2 * rows] + both[2 * rows :]
        cosine, sine = turn_ref[:rows], turn_ref[rows:]
        turned = []
        for block in (pair[:, :LANES], pair[:, LANES:], tap_out):
            real, imag = block[:rows], block[rows:]
            turned.append(jnp.concatenate([real * cosine + imag * sine, imag * cosine - real * sine], axis=1))
        work_h, work_l = split(jnp.concatenate(turned, axis=0))
        spec = dot(work_h, table(4)) + dot(work_l, table(4)) + dot(work_h, table(5))
        mix_re, mix_im = spec[:rows, :LANES], spec[:rows, LANES:]
        grad_re, grad_im = spec[rows : 2 * rows, :LANES], spec[rows : 2 * rows, LANES:]
        ker_re, ker_im = spec[2 * rows :, :LANES], spec[2 * rows :, LANES:]
        prods = jnp.concatenate(
            [
                jnp.concatenate([ker_re * mix_re - ker_im * mix_im, ker_re * mix_im + ker_im * mix_re], axis=1),
                jnp.concatenate([ker_re * grad_re + ker_im * grad_im, ker_re * grad_im - ker_im * grad_re], axis=1),
                jnp.concatenate([grad_re * mix_re + grad_im * mix_im, grad_im * mix_re - grad_re * mix_im], axis=1),
            ],
            axis=0,
        )
        prod_h, prod_l = split(prods)
        work = dot(prod_h, table(6)) + dot(prod_l, table(6)) + dot(prod_h, table(7))
        turned_re, turned_im = [], []
        for block in range(3):
            real = work[block * rows : (block + 1) * rows, :LANES]
            imag = work[block * rows : (block + 1) * rows, LANES:]
            turned_re.append(real * cosine - imag * sine)
            turned_im.append(imag * cosine + real * sine)
        real_h, real_l = split(jnp.concatenate(turned_re, axis=1))
        imag_h, imag_l = split(jnp.concatenate(turned_im, axis=1))
        result = dot(table(8), real_h) + dot(table(8), real_l) + dot(table(10), real_h)
        result = result + dot(table(9), imag_h) + dot(table(9), imag_l) + dot(table(11), imag_h)
        convolved, carried, lag_grad = [result[:, i * LANES : (i + 1) * LANES] for i in range(3)]

        gain = gain_ref[me * per + chan]
        grad_mixed = carried + gain * gated
        finals = (
            cot_f * (convolved + gain * mixed),
            grad_mixed * value_f,
            grad_mixed * key_f,
            lag_grad * norm_scale,
        )
        for slot, value in enumerate(finals):
            res_box[chan, :, slot] = value.astype(jnp.bfloat16).reshape(count, part, LANES)
        for step in reversed(range(1, count)):
            result_copy(chan, step).start()
        total = jnp.sum(jnp.sum(gated * mixed, axis=0, keepdims=True), axis=1, keepdims=True) * norm_scale
        sum_box[chan] = jnp.broadcast_to(total, (8, LANES))
        return carry

    lax.fori_loop(0, per, one_channel, 0)

    for step in range(1, count):
        sum_copy(step).start()
    for chan in range(per):
        got_box[me, chan] = res_box[chan, me]
    sum_got[me] = sum_box[...]
    for chan in range(per):
        for step in range(1, count):
            send_copy(chan, step).wait_send()
    for step in range(1, count):
        sum_copy(step).wait()
    for chan in range(per):
        for step in range(1, count):
            result_copy(chan, step).wait()

    for slot, ref in enumerate((gq_ref, gk_ref, gv_ref, gf_ref)):
        pieces = got_box[:, :, slot].reshape(chans, part, LANES).astype(jnp.float32)
        turned = jnp.swapaxes(pieces, 0, 1).astype(jnp.bfloat16)
        for r in range(part):
            ref[:, r * LANES : (r + 1) * LANES] = turned[r]
    skip_ref[...] = sum_got[...].reshape(chans, 8, LANES)[:, 0, :]


def local_channels(queries, key_proj, value_proj, cotangent, filter_taps, skip_gain):
    count = lax.axis_size("seq")
    chans, tok_local = queries.shape
    per = chans // count
    part = tok_local // LANES
    rows = part * count
    tables = transform_tables(rows)
    vmem = pl.BlockSpec(memory_space=pltpu.VMEM)
    hbm = pl.BlockSpec(memory_space=pltpu.HBM)
    smem = pl.BlockSpec(memory_space=pltpu.SMEM)
    block = jax.ShapeDtypeStruct((chans, tok_local), jnp.bfloat16)
    dma = pltpu.SemaphoreType.DMA
    *grads, skips = pl.pallas_call(
        functools.partial(channel_kernel, count),
        out_shape=[block] * 4 + [jax.ShapeDtypeStruct((chans, LANES), jnp.float32)],
        in_specs=[hbm] * 5 + [smem] + [hbm] * 2,
        out_specs=[vmem] * 5,
        scratch_shapes=[
            *[pltpu.VMEM((chans, tok_local), jnp.bfloat16) for _ in range(5)],
            *[pltpu.VMEM(table.shape, table.dtype) for table in tables],
            pltpu.VMEM((count, per, 5, part, LANES), jnp.bfloat16),
            pltpu.VMEM((per, count, 5, part, LANES), jnp.bfloat16),
            pltpu.VMEM((per, count, 4, part, LANES), jnp.bfloat16),
            pltpu.VMEM((count, per, 4, part, LANES), jnp.bfloat16),
            pltpu.VMEM((per, 8, LANES), jnp.float32),
            pltpu.VMEM((count, per, 8, LANES), jnp.float32),
            dma((per, count)),
            dma((per, count)),
            dma((per, count)),
            dma((per, count)),
            dma((count,)),
            dma((count,)),
            dma((7,)),
        ],
        compiler_params=pltpu.CompilerParams(
            collective_id=0, has_side_effects=True, vmem_limit_bytes=63 * 1024 * 1024
        ),
    )(queries, key_proj, value_proj, cotangent, filter_taps, skip_gain, *tables)
    return (*grads, skips[:, 0])


def local(*arguments):
    count = lax.axis_size("seq")
    chans, tok_local = arguments[0].shape
    whole_channels = chans % count == 0 and count & (count - 1) == 0
    if whole_channels and count > 1 and tok_local % (16 * LANES) == 0 and count * tok_local == 2 * LANES * LANES:
        return local_channels(*arguments)
    return local_butterfly(*arguments)


def solution(mesh):
    return jax.shard_map(
        local,
        mesh=mesh,
        in_specs=(
            P("chan", "seq"),
            P("chan", "seq"),
            P("chan", "seq"),
            P("chan", "seq"),
            P("chan", "seq"),
            P("chan"),
        ),
        out_specs=(
            P("chan", "seq"),
            P("chan", "seq"),
            P("chan", "seq"),
            P("chan", "seq"),
            P("chan"),
        ),
        check_vma=False,
    )
```

```python
import functools
import math

import jax
import jax.numpy as jnp
import ml_dtypes
import numpy as np
from jax import lax
from jax.experimental import pallas as pl
from jax.experimental.pallas import tpu as pltpu
from jax.sharding import PartitionSpec as P

highest = lax.Precision.HIGHEST


def from_partner(block, axis, stride):
    count = lax.axis_size(axis)
    route = []
    for low in range(count):
        high = low | 1 << stride
        if high != low and high < count:
            route += [(low, high), (high, low)]
    return lax.ppermute(block, axis, route)


def complex_product(pattern, left_re, left_im, right_re, right_im):
    real_real = jnp.einsum(pattern, left_re, right_re, precision=highest)
    imag_imag = jnp.einsum(pattern, left_im, right_im, precision=highest)
    real_imag = jnp.einsum(pattern, left_re, right_im, precision=highest)
    imag_real = jnp.einsum(pattern, left_im, right_re, precision=highest)
    return (real_real - imag_imag, real_imag + imag_real)


def rotate(real_in, imag_in, angle_val):
    cosine = jnp.cos(angle_val)
    sine_val = jnp.sin(angle_val)
    return (real_in * cosine - imag_in * sine_val, real_in * sine_val + imag_in * cosine)


def dft_table(length, direction):
    counter = jnp.arange(length, dtype=jnp.int32)
    phase_idx = counter[:, None] * counter[None, :] % length
    angle_val = direction * 2.0 * math.pi / length * phase_idx.astype(jnp.float32)
    return (jnp.cos(angle_val), jnp.sin(angle_val))


def twiddle_angle(row_count, radix_len, length, direction):
    phase_idx = (
        jnp.arange(row_count, dtype=jnp.int32)[:, None]
        * jnp.arange(radix_len, dtype=jnp.int32)[None, :]
        % length
    )
    return direction * 2.0 * math.pi / length * phase_idx.astype(jnp.float32)


def local_forward(real_in, imag_in):
    length = real_in.shape[-1]
    radix_len = math.gcd(length, 512)
    row_count = length // radix_len
    new_shape = real_in.shape[:-1] + (row_count, radix_len)
    first_re, first_im = dft_table(row_count, -1.0)
    work_re, work_im = complex_product(
        "ab,...bj->...aj",
        first_re,
        first_im,
        real_in.reshape(new_shape),
        imag_in.reshape(new_shape),
    )
    work_re, work_im = rotate(work_re, work_im, twiddle_angle(row_count, radix_len, length, -1.0))
    second_re, second_im = dft_table(radix_len, -1.0)
    work_re, work_im = complex_product("...aj,jk->...ak", work_re, work_im, second_re, second_im)
    return (work_re.reshape(real_in.shape), work_im.reshape(real_in.shape))


def local_inverse(real_in, imag_in):
    length = real_in.shape[-1]
    radix_len = math.gcd(length, 512)
    row_count = length // radix_len
    new_shape = real_in.shape[:-1] + (row_count, radix_len)
    second_re, second_im = dft_table(radix_len, 1.0)
    work_re, work_im = complex_product(
        "...ak,kj->...aj",
        real_in.reshape(new_shape),
        imag_in.reshape(new_shape),
        second_re,
        second_im,
    )
    work_re, work_im = rotate(work_re, work_im, twiddle_angle(row_count, radix_len, length, 1.0))
    first_re, first_im = dft_table(row_count, 1.0)
    work_re, work_im = complex_product("ab,...aj->...bj", first_re, first_im, work_re, work_im)
    return (work_re.reshape(real_in.shape), work_im.reshape(real_in.shape))


def bit_reverse(seq_index, bit_total):
    reversed_idx = jnp.zeros_like(seq_index)
    for bit_level in range(bit_total):
        reversed_idx = reversed_idx | (seq_index >> bit_level & 1) << bit_total - 1 - bit_level
    return reversed_idx


def frequency_angle(frequencies, lane_count, padded_len, direction):
    lanes = jnp.arange(lane_count, dtype=jnp.int32)
    parity = jnp.arange(2, dtype=jnp.int32)
    spectral = 2 * frequencies[None, :] + parity[:, None]
    phase_idx = spectral[:, :, None] * lanes[None, None, :] % padded_len
    angle_val = direction * 2.0 * math.pi / padded_len * phase_idx.astype(jnp.float32)
    return angle_val[:, None, None]


def to_spectrum(signals, blocks, seq_index, seq_count, block_total):
    lane_count = signals.shape[-1]
    padded_len = 2 * block_total * lane_count
    half_turn = (math.pi / block_total * blocks.astype(jnp.float32))[:, None]
    real_part = jnp.stack([signals, signals * jnp.cos(half_turn)])
    imag_part = jnp.stack([jnp.zeros_like(signals), -signals * jnp.sin(half_turn)])
    bit_total = seq_count.bit_length() - 1
    for bit_level in reversed(range(bit_total)):
        half_span = 1 << bit_level
        other_re, other_im = from_partner((real_part, imag_part), "seq", bit_level)
        position = seq_index % (2 * half_span)
        is_upper = position < half_span
        sum_re = jnp.where(is_upper, real_part + other_re, other_re - real_part)
        sum_im = jnp.where(is_upper, imag_part + other_im, other_im - imag_part)
        angle_val = jnp.where(
            is_upper, 0.0, -math.pi * (position % half_span).astype(jnp.float32) / half_span
        )
        real_part, imag_part = rotate(sum_re, sum_im, angle_val)
    frequencies = bit_reverse(seq_index, bit_total)[None]
    real_part, imag_part = rotate(
        real_part, imag_part, frequency_angle(frequencies, lane_count, padded_len, -1.0)
    )
    return (local_forward(real_part, imag_part), frequencies)


def to_signal(real_part, imag_part, frequencies, blocks, seq_index, seq_count, block_total):
    lane_count = real_part.shape[-1]
    padded_len = 2 * block_total * lane_count
    real_part, imag_part = local_inverse(real_part, imag_part)
    real_part, imag_part = rotate(
        real_part, imag_part, frequency_angle(frequencies, lane_count, padded_len, 1.0)
    )
    bit_total = seq_count.bit_length() - 1
    for bit_level in range(bit_total):
        half_span = 1 << bit_level
        other_re, other_im = from_partner((real_part, imag_part), "seq", bit_level)
        position = seq_index % (2 * half_span)
        is_upper = position < half_span
        taken_re = jnp.where(is_upper, other_re, real_part)
        taken_im = jnp.where(is_upper, other_im, imag_part)
        base_re = jnp.where(is_upper, real_part, other_re)
        base_im = jnp.where(is_upper, imag_part, other_im)
        angle_val = math.pi * (position % half_span).astype(jnp.float32) / half_span
        turned_re, turned_im = rotate(taken_re, taken_im, angle_val)
        flip_sign = jnp.where(is_upper, 1.0, -1.0)
        real_part = base_re + flip_sign * turned_re
        imag_part = base_im + flip_sign * turned_im
    half_turn = (math.pi / block_total * blocks.astype(jnp.float32))[:, None]
    combined = real_part[0] + real_part[1] * jnp.cos(half_turn) - imag_part[1] * jnp.sin(half_turn)
    return combined / padded_len


def local_butterfly(queries, key_proj, value_proj, cotangent, filter_taps, skip_gain):
    seq_count = lax.axis_size("seq")
    seq_index = lax.axis_index("seq")
    tok_local = queries.shape[1]
    tokens_all = seq_count * tok_local
    norm_scale = 1.0 / math.sqrt(tokens_all)
    chan_input = queries.shape[0]
    query_in, key_in, value_in, cot_in, taps_in = (
        queries,
        key_proj,
        value_proj,
        cotangent,
        filter_taps,
    )
    blocks = seq_index[None]
    block_shape = (chan_input, blocks.shape[0], tok_local)
    query_f = query_in.reshape(block_shape).astype(jnp.float32)
    key_f = key_in.reshape(block_shape).astype(jnp.float32)
    value_f = value_in.reshape(block_shape).astype(jnp.float32)
    cot_f = cot_in.reshape(block_shape).astype(jnp.float32)
    kernel = taps_in.reshape(block_shape).astype(jnp.float32)
    mixed = key_f * value_f
    gated = cot_f * query_f
    signals = jnp.stack([mixed, gated, kernel])
    (spec_re, spec_im), frequencies = to_spectrum(signals, blocks, seq_index, seq_count, seq_count)
    mix_re, mix_im = (spec_re[:, 0], spec_im[:, 0])
    grad_re, grad_im = (spec_re[:, 1], spec_im[:, 1])
    ker_re, ker_im = (spec_re[:, 2], spec_im[:, 2])
    prod_re = jnp.stack(
        [
            ker_re * mix_re - ker_im * mix_im,
            ker_re * grad_re + ker_im * grad_im,
            grad_re * mix_re + grad_im * mix_im,
        ],
        1,
    )
    prod_im = jnp.stack(
        [
            ker_re * mix_im + ker_im * mix_re,
            ker_re * grad_im - ker_im * grad_re,
            grad_im * mix_re - grad_re * mix_im,
        ],
        1,
    )
    results = to_signal(prod_re, prod_im, frequencies, blocks, seq_index, seq_count, seq_count)
    convolved, carried, lag_grad = (results[0], results[1], results[2])
    skip_col = skip_gain[:, None, None]
    grad_query = (cot_f * (convolved + skip_col * mixed)).astype(jnp.bfloat16)
    grad_mixed = carried + skip_col * gated
    grad_key = (grad_mixed * value_f).astype(jnp.bfloat16)
    grad_value = (grad_mixed * key_f).astype(jnp.bfloat16)
    grad_filter = (lag_grad * norm_scale).astype(jnp.bfloat16)
    skip_part = jnp.sum(gated * mixed, axis=(1, 2))
    flat_shape = (chan_input, tok_local)
    grad_query = grad_query.reshape(flat_shape)
    grad_key = grad_key.reshape(flat_shape)
    grad_value = grad_value.reshape(flat_shape)
    grad_filter = grad_filter.reshape(flat_shape)
    skip_sum = lax.psum(skip_part, "seq")
    return (grad_query, grad_key, grad_value, grad_filter, skip_sum * norm_scale)


LANES = 128


def halves(table):
    high = table.astype(np.float32).astype(ml_dtypes.bfloat16)
    low = (table - high.astype(np.float64)).astype(np.float32).astype(ml_dtypes.bfloat16)
    return high, low


def transform_tables(rows):
    total = rows * LANES
    quarter = np.arange(rows) + 0.25
    outer = 2.0 * np.pi / rows * np.outer(quarter, np.arange(rows))
    turn = 2.0 * np.pi / total * np.outer(quarter, np.arange(LANES))
    inner = 2.0 * np.pi / LANES * np.outer(np.arange(LANES), np.arange(LANES))
    first = np.concatenate([np.cos(outer), -np.sin(outer)], axis=0)
    second = np.block([[np.cos(inner), -np.sin(inner)], [np.sin(inner), np.cos(inner)]])
    second_back = np.block([[np.cos(inner), np.sin(inner)], [-np.sin(inner), np.cos(inner)]])
    first_back = np.concatenate([np.cos(outer.T), -np.sin(outer.T)], axis=1) / total
    parts = halves(first) + halves(second) + halves(second_back)
    for table in halves(first_back):
        parts += (table[:, :rows], table[:, rows:])
    turns = np.concatenate([np.cos(turn), np.sin(turn)]).astype(np.float32)
    return jnp.asarray(np.concatenate(parts)), jnp.asarray(turns)


def split(value):
    high = value.astype(jnp.bfloat16)
    low = (value - high.astype(jnp.float32)).astype(jnp.bfloat16)
    return high, low


def dot(left, right):
    return jnp.dot(left, right, preferred_element_type=jnp.float32)


def channel_kernel(
    count,
    *refs,
):
    args, gain_ref, tables, refs = refs[:5], refs[5], refs[6:8], refs[8:]
    got_box, sum_got = refs[:2]
    arg_vmem, table_vmem, refs = refs[2:7], refs[7:9], refs[9:]
    out_box, in_box, res_box, sum_box = refs[:4]
    send_in, recv_in, send_res, recv_res, send_sum, recv_sum, load_sem, own_sem = refs[4:]
    table_ref, turn_ref = table_vmem
    me = lax.axis_index("seq")
    chans, tok_local = args[0].shape
    per = chans // count
    part = tok_local // LANES
    rows = part * count
    norm_scale = 1.0 / math.sqrt(rows * LANES)

    barrier = pltpu.get_barrier_semaphore()
    for step in range(1, count):
        pl.semaphore_signal(barrier, inc=1, device_id={"seq": me ^ step}, device_id_type=pl.DeviceIdType.MESH)

    loads = [
        pltpu.make_async_copy(source, target, load_sem.at[i])
        for i, (source, target) in enumerate(zip(args + tables, arg_vmem + table_vmem))
    ]
    for load in loads[:5]:
        load.start()

    def peer_of(step):
        return me ^ step

    for load in loads[5:]:
        load.start()
    for slot, ref in enumerate(arg_vmem):
        loads[slot].wait()
        pieces = jnp.stack([ref[:, r * LANES : (r + 1) * LANES].astype(jnp.float32) for r in range(part)])
        turned = jnp.swapaxes(pieces, 0, 1).astype(jnp.bfloat16)
        out_box[:, :, slot] = turned.reshape(count, per, part, LANES)

    pl.semaphore_wait(barrier, count - 1)

    def send_copy(chan, step):
        peer = peer_of(step)
        return pltpu.make_async_remote_copy(
            src_ref=out_box.at[peer, chan],
            dst_ref=in_box.at[chan, me],
            send_sem=send_in.at[chan, step],
            recv_sem=recv_in.at[chan, step],
            device_id={"seq": peer},
            device_id_type=pl.DeviceIdType.MESH,
        )

    def result_copy(chan, step):
        peer = peer_of(step)
        return pltpu.make_async_remote_copy(
            src_ref=res_box.at[chan, peer],
            dst_ref=got_box.at[me, chan],
            send_sem=send_res.at[chan, step],
            recv_sem=recv_res.at[chan, step],
            device_id={"seq": peer},
            device_id_type=pl.DeviceIdType.MESH,
        )

    def own_result(chan):
        return pltpu.make_async_copy(res_box.at[chan, me], got_box.at[me, chan], own_sem.at[chan])

    def sum_copy(step):
        peer = peer_of(step)
        return pltpu.make_async_remote_copy(
            src_ref=sum_box,
            dst_ref=sum_got.at[me],
            send_sem=send_sum.at[step],
            recv_sem=recv_sum.at[step],
            device_id={"seq": peer},
            device_id_type=pl.DeviceIdType.MESH,
        )

    for chan in range(per):
        for step in reversed(range(1, count)):
            send_copy(chan, step).start()
    for chan in range(per):
        in_box[chan, me] = out_box[me, chan]

    query_f, key_f, value_f, cot_f = [ref[...].astype(jnp.float32) for ref in arg_vmem[:4]]
    column = jnp.sum((cot_f * query_f) * (key_f * value_f), axis=1, keepdims=True) * norm_scale
    lane = lax.broadcasted_iota(jnp.int32, (chans, LANES), 1)
    row = lax.broadcasted_iota(jnp.int32, (chans, LANES), 0)
    spread = jnp.sum(jnp.where(lane == row, column, 0.0), axis=0, keepdims=True)
    sum_box[...] = jnp.broadcast_to(spread, (8, LANES))
    for step in range(1, count):
        sum_copy(step).start()
    own_sum = pltpu.make_async_copy(sum_box, sum_got.at[me], own_sem.at[per])
    own_sum.start()

    for load in loads[5:]:
        load.wait()

    def table(first, blocks=1):
        return table_ref[first * rows : (first + blocks) * rows]

    def one_channel(chan, carry):
        for step in range(1, count):
            send_copy(chan, step).wait_recv()
        arrived = [in_box[chan, :, slot].reshape(rows, LANES) for slot in range(5)]
        query_f, key_f, value_f, cot_f = [a.astype(jnp.float32) for a in arrived[:4]]
        taps = arrived[4]
        mixed = key_f * value_f
        gated = cot_f * query_f
        mixed_h, mixed_l = split(mixed)
        gated_h, gated_l = split(gated)

        high = jnp.concatenate([mixed_h, gated_h], axis=1)
        low = jnp.concatenate([mixed_l, gated_l], axis=1)
        pair = dot(table(0, 2), high) + dot(table(0, 2), low) + dot(table(2, 2), high)
        both = dot(table(0, 4), taps)
        tap_out = both[: 2 * rows] + both[2 * rows :]
        cosine, sine = turn_ref[:rows], turn_ref[rows:]
        turned = []
        for block in (pair[:, :LANES], pair[:, LANES:], tap_out):
            real, imag = block[:rows], block[rows:]
            turned.append(jnp.concatenate([real * cosine + imag * sine, imag * cosine - real * sine], axis=1))
        work_h, work_l = split(jnp.concatenate(turned, axis=0))
        spec = dot(work_h, table(4)) + dot(work_l, table(4)) + dot(work_h, table(5))
        mix_re, mix_im = spec[:rows, :LANES], spec[:rows, LANES:]
        grad_re, grad_im = spec[rows : 2 * rows, :LANES], spec[rows : 2 * rows, LANES:]
        ker_re, ker_im = spec[2 * rows :, :LANES], spec[2 * rows :, LANES:]
        prods = jnp.concatenate(
            [
                jnp.concatenate([ker_re * mix_re - ker_im * mix_im, ker_re * mix_im + ker_im * mix_re], axis=1),
                jnp.concatenate([ker_re * grad_re + ker_im * grad_im, ker_re * grad_im - ker_im * grad_re], axis=1),
                jnp.concatenate([grad_re * mix_re + grad_im * mix_im, grad_im * mix_re - grad_re * mix_im], axis=1),
            ],
            axis=0,
        )
        prod_h, prod_l = split(prods)
        work = dot(prod_h, table(6)) + dot(prod_l, table(6)) + dot(prod_h, table(7))
        turned_re, turned_im = [], []
        for block in range(3):
            real = work[block * rows : (block + 1) * rows, :LANES]
            imag = work[block * rows : (block + 1) * rows, LANES:]
            turned_re.append(real * cosine - imag * sine)
            turned_im.append(imag * cosine + real * sine)
        real_h, real_l = split(jnp.concatenate(turned_re, axis=1))
        imag_h, imag_l = split(jnp.concatenate(turned_im, axis=1))
        result = dot(table(8), real_h) + dot(table(8), real_l) + dot(table(10), real_h)
        result = result + dot(table(9), imag_h) + dot(table(9), imag_l) + dot(table(11), imag_h)
        convolved, carried, lag_grad = [result[:, i * LANES : (i + 1) * LANES] for i in range(3)]

        gain = gain_ref[me * per + chan]
        grad_mixed = carried + gain * gated
        finals = (
            cot_f * (convolved + gain * mixed),
            grad_mixed * value_f,
            grad_mixed * key_f,
            lag_grad * norm_scale,
        )
        for slot, value in enumerate(finals):
            res_box[chan, :, slot] = value.astype(jnp.bfloat16).reshape(count, part, LANES)
        for step in reversed(range(1, count)):
            result_copy(chan, step).start()
        own_result(chan).start()
        return carry

    lax.fori_loop(0, per, one_channel, 0)

    for chan in range(per):
        for step in range(1, count):
            send_copy(chan, step).wait_send()
    own_sum.wait()
    for step in range(1, count):
        sum_copy(step).wait()
    for chan in range(per):
        own_result(chan).wait()
        for step in range(1, count):
            result_copy(chan, step).wait()


def finish_kernel(got_ref, sum_ref, *refs):
    outs, skip_ref = refs[:4], refs[4]
    got_vmem, out_vmem, load_sem, store_sem = refs[5:]
    count, per, _, part, _ = got_ref.shape
    chans = count * per
    loads = [
        pltpu.make_async_copy(got_ref.at[:, :, slot], got_vmem.at[slot], load_sem.at[slot]) for slot in range(4)
    ]
    stores = [pltpu.make_async_copy(out_vmem.at[slot], outs[slot], store_sem.at[slot]) for slot in range(4)]
    for load in loads:
        load.start()
    skip_ref[...] = jnp.sum(sum_ref[...], axis=0)[0, :chans]
    for slot in range(4):
        loads[slot].wait()
        pieces = got_vmem[slot].reshape(chans, part, LANES).astype(jnp.float32)
        turned = jnp.swapaxes(pieces, 0, 1).astype(jnp.bfloat16)
        for r in range(part):
            out_vmem[slot, :, r * LANES : (r + 1) * LANES] = turned[r]
        stores[slot].start()
    for store in stores:
        store.wait()


def local_channels(queries, key_proj, value_proj, cotangent, filter_taps, skip_gain):
    count = lax.axis_size("seq")
    chans, tok_local = queries.shape
    per = chans // count
    part = tok_local // LANES
    rows = part * count
    tables = transform_tables(rows)
    vmem = pl.BlockSpec(memory_space=pltpu.VMEM)
    hbm = pl.BlockSpec(memory_space=pltpu.HBM)
    smem = pl.BlockSpec(memory_space=pltpu.SMEM)
    block = jax.ShapeDtypeStruct((chans, tok_local), jnp.bfloat16)
    dma = pltpu.SemaphoreType.DMA
    got, sums = pl.pallas_call(
        functools.partial(channel_kernel, count),
        out_shape=[
            jax.ShapeDtypeStruct((count, per, 4, part, LANES), jnp.bfloat16),
            jax.ShapeDtypeStruct((count, 8, LANES), jnp.float32),
        ],
        in_specs=[hbm] * 5 + [smem] + [hbm] * 2,
        out_specs=[hbm] * 2,
        scratch_shapes=[
            *[pltpu.VMEM((chans, tok_local), jnp.bfloat16) for _ in range(5)],
            *[pltpu.VMEM(table.shape, table.dtype) for table in tables],
            pltpu.VMEM((count, per, 5, part, LANES), jnp.bfloat16),
            pltpu.VMEM((per, count, 5, part, LANES), jnp.bfloat16),
            pltpu.VMEM((per, count, 4, part, LANES), jnp.bfloat16),
            pltpu.VMEM((8, LANES), jnp.float32),
            dma((per, count)),
            dma((per, count)),
            dma((per, count)),
            dma((per, count)),
            dma((count,)),
            dma((count,)),
            dma((7,)),
            dma((per + 1,)),
        ],
        compiler_params=pltpu.CompilerParams(
            collective_id=0, has_side_effects=True, vmem_limit_bytes=63 * 1024 * 1024
        ),
    )(queries, key_proj, value_proj, cotangent, filter_taps, skip_gain, *tables)
    return pl.pallas_call(
        finish_kernel,
        out_shape=[block] * 4 + [jax.ShapeDtypeStruct((chans,), jnp.float32)],
        in_specs=[hbm, vmem],
        out_specs=[hbm] * 4 + [vmem],
        scratch_shapes=[
            pltpu.VMEM((4, count, per, part, LANES), jnp.bfloat16),
            pltpu.VMEM((4, chans, tok_local), jnp.bfloat16),
            dma((4,)),
            dma((4,)),
        ],
        compiler_params=pltpu.CompilerParams(vmem_limit_bytes=63 * 1024 * 1024),
    )(got, sums)


def local(*arguments):
    count = lax.axis_size("seq")
    chans, tok_local = arguments[0].shape
    whole_channels = chans % count == 0 and count & (count - 1) == 0
    if whole_channels and count > 1 and tok_local % (16 * LANES) == 0 and count * tok_local == 2 * LANES * LANES:
        return local_channels(*arguments)
    return local_butterfly(*arguments)


def solution(mesh):
    return jax.shard_map(
        local,
        mesh=mesh,
        in_specs=(
            P("chan", "seq"),
            P("chan", "seq"),
            P("chan", "seq"),
            P("chan", "seq"),
            P("chan", "seq"),
            P("chan"),
        ),
        out_specs=(
            P("chan", "seq"),
            P("chan", "seq"),
            P("chan", "seq"),
            P("chan", "seq"),
            P("chan"),
        ),
        check_vma=False,
    )
```

```python
import functools
import math

import jax
import jax.numpy as jnp
import ml_dtypes
import numpy as np
from jax import lax
from jax.experimental import pallas as pl
from jax.experimental.pallas import tpu as pltpu
from jax.sharding import PartitionSpec as P

highest = lax.Precision.HIGHEST


def from_partner(block, axis, stride):
    count = lax.axis_size(axis)
    route = []
    for low in range(count):
        high = low | 1 << stride
        if high != low and high < count:
            route += [(low, high), (high, low)]
    return lax.ppermute(block, axis, route)


def complex_product(pattern, left_re, left_im, right_re, right_im):
    real_real = jnp.einsum(pattern, left_re, right_re, precision=highest)
    imag_imag = jnp.einsum(pattern, left_im, right_im, precision=highest)
    real_imag = jnp.einsum(pattern, left_re, right_im, precision=highest)
    imag_real = jnp.einsum(pattern, left_im, right_re, precision=highest)
    return (real_real - imag_imag, real_imag + imag_real)


def rotate(real_in, imag_in, angle_val):
    cosine = jnp.cos(angle_val)
    sine_val = jnp.sin(angle_val)
    return (real_in * cosine - imag_in * sine_val, real_in * sine_val + imag_in * cosine)


def dft_table(length, direction):
    counter = jnp.arange(length, dtype=jnp.int32)
    phase_idx = counter[:, None] * counter[None, :] % length
    angle_val = direction * 2.0 * math.pi / length * phase_idx.astype(jnp.float32)
    return (jnp.cos(angle_val), jnp.sin(angle_val))


def twiddle_angle(row_count, radix_len, length, direction):
    phase_idx = (
        jnp.arange(row_count, dtype=jnp.int32)[:, None]
        * jnp.arange(radix_len, dtype=jnp.int32)[None, :]
        % length
    )
    return direction * 2.0 * math.pi / length * phase_idx.astype(jnp.float32)


def local_forward(real_in, imag_in):
    length = real_in.shape[-1]
    radix_len = math.gcd(length, 512)
    row_count = length // radix_len
    new_shape = real_in.shape[:-1] + (row_count, radix_len)
    first_re, first_im = dft_table(row_count, -1.0)
    work_re, work_im = complex_product(
        "ab,...bj->...aj",
        first_re,
        first_im,
        real_in.reshape(new_shape),
        imag_in.reshape(new_shape),
    )
    work_re, work_im = rotate(work_re, work_im, twiddle_angle(row_count, radix_len, length, -1.0))
    second_re, second_im = dft_table(radix_len, -1.0)
    work_re, work_im = complex_product("...aj,jk->...ak", work_re, work_im, second_re, second_im)
    return (work_re.reshape(real_in.shape), work_im.reshape(real_in.shape))


def local_inverse(real_in, imag_in):
    length = real_in.shape[-1]
    radix_len = math.gcd(length, 512)
    row_count = length // radix_len
    new_shape = real_in.shape[:-1] + (row_count, radix_len)
    second_re, second_im = dft_table(radix_len, 1.0)
    work_re, work_im = complex_product(
        "...ak,kj->...aj",
        real_in.reshape(new_shape),
        imag_in.reshape(new_shape),
        second_re,
        second_im,
    )
    work_re, work_im = rotate(work_re, work_im, twiddle_angle(row_count, radix_len, length, 1.0))
    first_re, first_im = dft_table(row_count, 1.0)
    work_re, work_im = complex_product("ab,...aj->...bj", first_re, first_im, work_re, work_im)
    return (work_re.reshape(real_in.shape), work_im.reshape(real_in.shape))


def bit_reverse(seq_index, bit_total):
    reversed_idx = jnp.zeros_like(seq_index)
    for bit_level in range(bit_total):
        reversed_idx = reversed_idx | (seq_index >> bit_level & 1) << bit_total - 1 - bit_level
    return reversed_idx


def frequency_angle(frequencies, lane_count, padded_len, direction):
    lanes = jnp.arange(lane_count, dtype=jnp.int32)
    parity = jnp.arange(2, dtype=jnp.int32)
    spectral = 2 * frequencies[None, :] + parity[:, None]
    phase_idx = spectral[:, :, None] * lanes[None, None, :] % padded_len
    angle_val = direction * 2.0 * math.pi / padded_len * phase_idx.astype(jnp.float32)
    return angle_val[:, None, None]


def to_spectrum(signals, blocks, seq_index, seq_count, block_total):
    lane_count = signals.shape[-1]
    padded_len = 2 * block_total * lane_count
    half_turn = (math.pi / block_total * blocks.astype(jnp.float32))[:, None]
    real_part = jnp.stack([signals, signals * jnp.cos(half_turn)])
    imag_part = jnp.stack([jnp.zeros_like(signals), -signals * jnp.sin(half_turn)])
    bit_total = seq_count.bit_length() - 1
    for bit_level in reversed(range(bit_total)):
        half_span = 1 << bit_level
        other_re, other_im = from_partner((real_part, imag_part), "seq", bit_level)
        position = seq_index % (2 * half_span)
        is_upper = position < half_span
        sum_re = jnp.where(is_upper, real_part + other_re, other_re - real_part)
        sum_im = jnp.where(is_upper, imag_part + other_im, other_im - imag_part)
        angle_val = jnp.where(
            is_upper, 0.0, -math.pi * (position % half_span).astype(jnp.float32) / half_span
        )
        real_part, imag_part = rotate(sum_re, sum_im, angle_val)
    frequencies = bit_reverse(seq_index, bit_total)[None]
    real_part, imag_part = rotate(
        real_part, imag_part, frequency_angle(frequencies, lane_count, padded_len, -1.0)
    )
    return (local_forward(real_part, imag_part), frequencies)


def to_signal(real_part, imag_part, frequencies, blocks, seq_index, seq_count, block_total):
    lane_count = real_part.shape[-1]
    padded_len = 2 * block_total * lane_count
    real_part, imag_part = local_inverse(real_part, imag_part)
    real_part, imag_part = rotate(
        real_part, imag_part, frequency_angle(frequencies, lane_count, padded_len, 1.0)
    )
    bit_total = seq_count.bit_length() - 1
    for bit_level in range(bit_total):
        half_span = 1 << bit_level
        other_re, other_im = from_partner((real_part, imag_part), "seq", bit_level)
        position = seq_index % (2 * half_span)
        is_upper = position < half_span
        taken_re = jnp.where(is_upper, other_re, real_part)
        taken_im = jnp.where(is_upper, other_im, imag_part)
        base_re = jnp.where(is_upper, real_part, other_re)
        base_im = jnp.where(is_upper, imag_part, other_im)
        angle_val = math.pi * (position % half_span).astype(jnp.float32) / half_span
        turned_re, turned_im = rotate(taken_re, taken_im, angle_val)
        flip_sign = jnp.where(is_upper, 1.0, -1.0)
        real_part = base_re + flip_sign * turned_re
        imag_part = base_im + flip_sign * turned_im
    half_turn = (math.pi / block_total * blocks.astype(jnp.float32))[:, None]
    combined = real_part[0] + real_part[1] * jnp.cos(half_turn) - imag_part[1] * jnp.sin(half_turn)
    return combined / padded_len


def local_butterfly(queries, key_proj, value_proj, cotangent, filter_taps, skip_gain):
    seq_count = lax.axis_size("seq")
    seq_index = lax.axis_index("seq")
    tok_local = queries.shape[1]
    tokens_all = seq_count * tok_local
    norm_scale = 1.0 / math.sqrt(tokens_all)
    chan_input = queries.shape[0]
    query_in, key_in, value_in, cot_in, taps_in = (
        queries,
        key_proj,
        value_proj,
        cotangent,
        filter_taps,
    )
    blocks = seq_index[None]
    block_shape = (chan_input, blocks.shape[0], tok_local)
    query_f = query_in.reshape(block_shape).astype(jnp.float32)
    key_f = key_in.reshape(block_shape).astype(jnp.float32)
    value_f = value_in.reshape(block_shape).astype(jnp.float32)
    cot_f = cot_in.reshape(block_shape).astype(jnp.float32)
    kernel = taps_in.reshape(block_shape).astype(jnp.float32)
    mixed = key_f * value_f
    gated = cot_f * query_f
    signals = jnp.stack([mixed, gated, kernel])
    (spec_re, spec_im), frequencies = to_spectrum(signals, blocks, seq_index, seq_count, seq_count)
    mix_re, mix_im = (spec_re[:, 0], spec_im[:, 0])
    grad_re, grad_im = (spec_re[:, 1], spec_im[:, 1])
    ker_re, ker_im = (spec_re[:, 2], spec_im[:, 2])
    prod_re = jnp.stack(
        [
            ker_re * mix_re - ker_im * mix_im,
            ker_re * grad_re + ker_im * grad_im,
            grad_re * mix_re + grad_im * mix_im,
        ],
        1,
    )
    prod_im = jnp.stack(
        [
            ker_re * mix_im + ker_im * mix_re,
            ker_re * grad_im - ker_im * grad_re,
            grad_im * mix_re - grad_re * mix_im,
        ],
        1,
    )
    results = to_signal(prod_re, prod_im, frequencies, blocks, seq_index, seq_count, seq_count)
    convolved, carried, lag_grad = (results[0], results[1], results[2])
    skip_col = skip_gain[:, None, None]
    grad_query = (cot_f * (convolved + skip_col * mixed)).astype(jnp.bfloat16)
    grad_mixed = carried + skip_col * gated
    grad_key = (grad_mixed * value_f).astype(jnp.bfloat16)
    grad_value = (grad_mixed * key_f).astype(jnp.bfloat16)
    grad_filter = (lag_grad * norm_scale).astype(jnp.bfloat16)
    skip_part = jnp.sum(gated * mixed, axis=(1, 2))
    flat_shape = (chan_input, tok_local)
    grad_query = grad_query.reshape(flat_shape)
    grad_key = grad_key.reshape(flat_shape)
    grad_value = grad_value.reshape(flat_shape)
    grad_filter = grad_filter.reshape(flat_shape)
    skip_sum = lax.psum(skip_part, "seq")
    return (grad_query, grad_key, grad_value, grad_filter, skip_sum * norm_scale)


LANES = 128


def halves(table):
    high = table.astype(np.float32).astype(ml_dtypes.bfloat16)
    low = (table - high.astype(np.float64)).astype(np.float32).astype(ml_dtypes.bfloat16)
    return high, low


def transform_tables(rows):
    total = rows * LANES
    quarter = np.arange(rows) + 0.25
    outer = 2.0 * np.pi / rows * np.outer(quarter, np.arange(rows))
    turn = 2.0 * np.pi / total * np.outer(quarter, np.arange(LANES))
    inner = 2.0 * np.pi / LANES * np.outer(np.arange(LANES), np.arange(LANES))
    first = np.concatenate([np.cos(outer), -np.sin(outer)], axis=0)
    second = np.block([[np.cos(inner), -np.sin(inner)], [np.sin(inner), np.cos(inner)]])
    second_back = np.block([[np.cos(inner), np.sin(inner)], [-np.sin(inner), np.cos(inner)]])
    first_back = np.concatenate([np.cos(outer.T), -np.sin(outer.T)], axis=1) / total
    parts = halves(first) + halves(second) + halves(second_back)
    for table in halves(first_back):
        parts += (table[:, :rows], table[:, rows:])
    turns = np.concatenate([np.cos(turn), np.sin(turn)]).astype(np.float32)
    return jnp.asarray(np.concatenate(parts)), jnp.asarray(turns)


def split(value):
    high = value.astype(jnp.bfloat16)
    low = (value - high.astype(jnp.float32)).astype(jnp.bfloat16)
    return high, low


def dot(left, right):
    return jnp.dot(left, right, preferred_element_type=jnp.float32)


def channel_kernel(
    count,
    *refs,
):
    args, gain_ref, tables, refs = refs[:5], refs[5], refs[6:8], refs[8:]
    got_box, sum_got = refs[:2]
    arg_vmem, table_vmem, refs = refs[2:7], refs[7:9], refs[9:]
    out_box, in_box, res_box, sum_box = refs[:4]
    send_in, recv_in, send_res, recv_res, send_sum, recv_sum, load_sem, own_sem = refs[4:]
    table_ref, turn_ref = table_vmem
    me = lax.axis_index("seq")
    chans, tok_local = args[0].shape
    per = chans // count
    part = tok_local // LANES
    rows = part * count
    norm_scale = 1.0 / math.sqrt(rows * LANES)

    barrier = pltpu.get_barrier_semaphore()
    for step in range(1, count):
        pl.semaphore_signal(barrier, inc=1, device_id={"seq": me ^ step}, device_id_type=pl.DeviceIdType.MESH)

    loads = [
        pltpu.make_async_copy(source, target, load_sem.at[i])
        for i, (source, target) in enumerate(zip(args + tables, arg_vmem + table_vmem))
    ]
    for load in loads[:5]:
        load.start()

    def peer_of(step):
        return me ^ step

    for load in loads[5:]:
        load.start()
    for slot, ref in enumerate(arg_vmem):
        loads[slot].wait()
        pieces = jnp.stack([ref[:, r * LANES : (r + 1) * LANES].astype(jnp.float32) for r in range(part)])
        turned = jnp.swapaxes(pieces, 0, 1).astype(jnp.bfloat16)
        out_box[:, :, slot] = turned.reshape(count, per, part, LANES)

    pl.semaphore_wait(barrier, count - 1)

    def send_copy(chan, step):
        peer = peer_of(step)
        return pltpu.make_async_remote_copy(
            src_ref=out_box.at[peer, chan],
            dst_ref=in_box.at[chan, me],
            send_sem=send_in.at[chan, step],
            recv_sem=recv_in.at[chan, step],
            device_id={"seq": peer},
            device_id_type=pl.DeviceIdType.MESH,
        )

    def result_copy(chan, step):
        peer = peer_of(step)
        return pltpu.make_async_remote_copy(
            src_ref=res_box.at[chan, peer],
            dst_ref=got_box.at[me, chan],
            send_sem=send_res.at[chan, step],
            recv_sem=recv_res.at[chan, step],
            device_id={"seq": peer},
            device_id_type=pl.DeviceIdType.MESH,
        )

    def own_result(chan):
        return pltpu.make_async_copy(res_box.at[chan, me], got_box.at[me, chan], own_sem.at[chan])

    def sum_copy(step):
        peer = peer_of(step)
        return pltpu.make_async_remote_copy(
            src_ref=sum_box,
            dst_ref=sum_got.at[me],
            send_sem=send_sum.at[step],
            recv_sem=recv_sum.at[step],
            device_id={"seq": peer},
            device_id_type=pl.DeviceIdType.MESH,
        )

    for chan in range(per):
        for step in reversed(range(1, count)):
            send_copy(chan, step).start()
    for chan in range(per):
        in_box[chan, me] = out_box[me, chan]

    query_f, key_f, value_f, cot_f = [ref[...].astype(jnp.float32) for ref in arg_vmem[:4]]
    column = jnp.sum((cot_f * query_f) * (key_f * value_f), axis=1, keepdims=True) * norm_scale
    lane = lax.broadcasted_iota(jnp.int32, (chans, LANES), 1)
    row = lax.broadcasted_iota(jnp.int32, (chans, LANES), 0)
    spread = jnp.sum(jnp.where(lane == row, column, 0.0), axis=0, keepdims=True)
    sum_box[...] = jnp.broadcast_to(spread, (8, LANES))
    for step in range(1, count):
        sum_copy(step).start()
    own_sum = pltpu.make_async_copy(sum_box, sum_got.at[me], own_sem.at[per])
    own_sum.start()

    for load in loads[5:]:
        load.wait()

    def table(first, blocks=1):
        return table_ref[first * rows : (first + blocks) * rows]

    def one_channel(chan, carry):
        for step in range(1, count):
            send_copy(chan, step).wait_recv()
        arrived = [in_box[chan, :, slot].reshape(rows, LANES) for slot in range(5)]
        query_f, key_f, value_f, cot_f = [a.astype(jnp.float32) for a in arrived[:4]]
        taps = arrived[4]
        mixed = key_f * value_f
        gated = cot_f * query_f
        mixed_h, mixed_l = split(mixed)
        gated_h, gated_l = split(gated)

        high = jnp.concatenate([mixed_h, gated_h], axis=1)
        low = jnp.concatenate([mixed_l, gated_l], axis=1)
        pair = dot(table(0, 2), high) + dot(table(0, 2), low) + dot(table(2, 2), high)
        both = dot(table(0, 4), taps)
        tap_out = both[: 2 * rows] + both[2 * rows :]
        cosine, sine = turn_ref[:rows], turn_ref[rows:]
        turned = []
        for block in (pair[:, :LANES], pair[:, LANES:], tap_out):
            real, imag = block[:rows], block[rows:]
            turned.append(jnp.concatenate([real * cosine + imag * sine, imag * cosine - real * sine], axis=1))
        work_h, work_l = split(jnp.concatenate(turned, axis=0))
        spec = dot(work_h, table(4)) + dot(work_l, table(4)) + dot(work_h, table(5))
        mix_re, mix_im = spec[:rows, :LANES], spec[:rows, LANES:]
        grad_re, grad_im = spec[rows : 2 * rows, :LANES], spec[rows : 2 * rows, LANES:]
        ker_re, ker_im = spec[2 * rows :, :LANES], spec[2 * rows :, LANES:]
        prods = jnp.concatenate(
            [
                jnp.concatenate([ker_re * mix_re - ker_im * mix_im, ker_re * mix_im + ker_im * mix_re], axis=1),
                jnp.concatenate([ker_re * grad_re + ker_im * grad_im, ker_re * grad_im - ker_im * grad_re], axis=1),
                jnp.concatenate([grad_re * mix_re + grad_im * mix_im, grad_im * mix_re - grad_re * mix_im], axis=1),
            ],
            axis=0,
        )
        prod_h, prod_l = split(prods)
        work = dot(prod_h, table(6)) + dot(prod_l, table(6)) + dot(prod_h, table(7))
        turned_re, turned_im = [], []
        for block in range(3):
            real = work[block * rows : (block + 1) * rows, :LANES]
            imag = work[block * rows : (block + 1) * rows, LANES:]
            turned_re.append(real * cosine - imag * sine)
            turned_im.append(imag * cosine + real * sine)
        real_h, real_l = split(jnp.concatenate(turned_re, axis=1))
        imag_h, imag_l = split(jnp.concatenate(turned_im, axis=1))
        result = dot(table(8), real_h) + dot(table(8), real_l) + dot(table(10), real_h)
        result = result + dot(table(9), imag_h) + dot(table(9), imag_l) + dot(table(11), imag_h)
        convolved, carried, lag_grad = [result[:, i * LANES : (i + 1) * LANES] for i in range(3)]

        gain = gain_ref[me * per + chan]
        grad_mixed = carried + gain * gated
        finals = (
            cot_f * (convolved + gain * mixed),
            grad_mixed * value_f,
            grad_mixed * key_f,
            lag_grad * norm_scale,
        )
        for slot, value in enumerate(finals):
            res_box[chan, :, slot] = value.astype(jnp.bfloat16).reshape(count, part, LANES)
        for step in reversed(range(1, count)):
            result_copy(chan, step).start()
        own_result(chan).start()
        return carry

    lax.fori_loop(0, per, one_channel, 0)

    for chan in range(per):
        for step in range(1, count):
            send_copy(chan, step).wait_send()
    own_sum.wait()
    for step in range(1, count):
        sum_copy(step).wait()
    for chan in range(per):
        own_result(chan).wait()
        for step in range(1, count):
            result_copy(chan, step).wait()


def finish_kernel(got_ref, sum_ref, *refs):
    outs, skip_ref = refs[:4], refs[4]
    out_vmem, store_sem = refs[5:]
    count, per, _, part, _ = got_ref.shape
    chans = count * per
    stores = [pltpu.make_async_copy(out_vmem.at[slot], outs[slot], store_sem.at[slot]) for slot in range(4)]
    skip_ref[...] = jnp.sum(sum_ref[...], axis=0)[0, :chans]
    for slot in range(4):
        pieces = got_ref[:, :, slot].reshape(chans, part, LANES).astype(jnp.float32)
        turned = jnp.swapaxes(pieces, 0, 1).astype(jnp.bfloat16)
        for r in range(part):
            out_vmem[slot, :, r * LANES : (r + 1) * LANES] = turned[r]
        stores[slot].start()
    for store in stores:
        store.wait()


def local_channels(queries, key_proj, value_proj, cotangent, filter_taps, skip_gain):
    count = lax.axis_size("seq")
    chans, tok_local = queries.shape
    per = chans // count
    part = tok_local // LANES
    rows = part * count
    tables = transform_tables(rows)
    vmem = pl.BlockSpec(memory_space=pltpu.VMEM)
    hbm = pl.BlockSpec(memory_space=pltpu.HBM)
    smem = pl.BlockSpec(memory_space=pltpu.SMEM)
    block = jax.ShapeDtypeStruct((chans, tok_local), jnp.bfloat16)
    dma = pltpu.SemaphoreType.DMA
    got, sums = pl.pallas_call(
        functools.partial(channel_kernel, count),
        out_shape=[
            pltpu.VMEM((count, per, 4, part, LANES), jnp.bfloat16),
            pltpu.VMEM((count, 8, LANES), jnp.float32),
        ],
        in_specs=[hbm] * 5 + [smem] + [hbm] * 2,
        out_specs=[vmem] * 2,
        scratch_shapes=[
            *[pltpu.VMEM((chans, tok_local), jnp.bfloat16) for _ in range(5)],
            *[pltpu.VMEM(table.shape, table.dtype) for table in tables],
            pltpu.VMEM((count, per, 5, part, LANES), jnp.bfloat16),
            pltpu.VMEM((per, count, 5, part, LANES), jnp.bfloat16),
            pltpu.VMEM((per, count, 4, part, LANES), jnp.bfloat16),
            pltpu.VMEM((8, LANES), jnp.float32),
            dma((per, count)),
            dma((per, count)),
            dma((per, count)),
            dma((per, count)),
            dma((count,)),
            dma((count,)),
            dma((7,)),
            dma((per + 1,)),
        ],
        compiler_params=pltpu.CompilerParams(
            collective_id=0, has_side_effects=True, vmem_limit_bytes=(64 * 1024 - 896) * 1024
        ),
    )(queries, key_proj, value_proj, cotangent, filter_taps, skip_gain, *tables)
    return pl.pallas_call(
        finish_kernel,
        out_shape=[block] * 4 + [jax.ShapeDtypeStruct((chans,), jnp.float32)],
        in_specs=[vmem, vmem],
        out_specs=[hbm] * 4 + [vmem],
        scratch_shapes=[
            pltpu.VMEM((4, chans, tok_local), jnp.bfloat16),
            dma((4,)),
        ],
        compiler_params=pltpu.CompilerParams(vmem_limit_bytes=32 * 1024 * 1024),
    )(got, sums)


def local(*arguments):
    count = lax.axis_size("seq")
    chans, tok_local = arguments[0].shape
    whole_channels = chans % count == 0 and count & (count - 1) == 0
    if whole_channels and count > 1 and tok_local % (16 * LANES) == 0 and count * tok_local == 2 * LANES * LANES:
        return local_channels(*arguments)
    return local_butterfly(*arguments)


def solution(mesh):
    return jax.shard_map(
        local,
        mesh=mesh,
        in_specs=(
            P("chan", "seq"),
            P("chan", "seq"),
            P("chan", "seq"),
            P("chan", "seq"),
            P("chan", "seq"),
            P("chan"),
        ),
        out_specs=(
            P("chan", "seq"),
            P("chan", "seq"),
            P("chan", "seq"),
            P("chan", "seq"),
            P("chan"),
        ),
        check_vma=False,
    )
```
